256 devices in a mesh: row: 32 (over z, y_hi, core), col: 8 (over y_lo, x).
Axes of the slice: x: 4, y: 4 (y_hi: 2, y_lo: 2; y = y_hi * 2 + y_lo), z: 8, core: 2. Of those that a mesh axis runs over, the one named last changes fastest.
Arguments:
- features: bfloat16 [512, 512, 384], P('row', 'col'), may hold values from -30 to 30
- inner_weights: bfloat16 [4, 3, 3, 384, 384], replicated, may hold values from -0.109375 to 0.109375
- far_weights: bfloat16 [3, 3, 384, 384], replicated, may hold values from -0.109375 to 0.109375
- gains: float32 [5, 384], replicated, may hold values from 0.1 to 1.9
Outputs:
- result: float32 [512, 512, 384], P('row', 'col')
The draws below stay inside these ranges and needn't reach their ends.
All inputs are finite; a program needn't handle non-finite values.
Results may differ from the reference program's by a relative error of at most 0.0024.
Values may be sent and summed in bfloat16 or wider, within the bound.
A program may use at most 192 MiB of HBM per device.

```python
import math
import jax
import jax.numpy as jnp
from jax import lax

CH = 384
LAYERS = 4
FAR = 64
HEIGHT = 512
WIDTH = 512


def draw_features(key, part):
    key_base, key_chan, key_cell = jax.random.split(key, 3)
    channel_scale = jnp.exp(jax.random.uniform(key_chan, (CH,), jnp.float32, math.log(0.3), math.log(3.0)))
    cell_scale = jnp.exp(jax.random.uniform(key_cell, (HEIGHT, WIDTH, 1), jnp.float32, math.log(0.5), math.log(2.0)))
    base_values = jnp.clip(jax.random.normal(key_base, (HEIGHT, WIDTH, CH), jnp.float32), -5.0, 5.0)
    return (base_values * channel_scale * cell_scale).astype(jnp.bfloat16)


def normal_values(stream_key, shape, deviation, most, kind=jnp.bfloat16):
    result = deviation * jax.random.normal(stream_key, shape, jnp.float32)
    return jnp.clip(result, min=-most, max=most).astype(kind)


def setup_inputs(seed: int = 0) -> dict:
    splits = jax.random.split(jax.random.key(seed), 5)
    return {
        "features": draw_features(jax.random.fold_in(splits[4], 71), 0),
        "inner_weights": normal_values(splits[1], (LAYERS, 3, 3, CH, CH), (9 * CH) ** -0.5, 0.109375),
        "far_weights": normal_values(splits[2], (3, 3, CH, CH), (9 * CH) ** -0.5, 0.109375),
        "gains": jnp.clip(1.0 + 0.18 * jax.random.normal(splits[3], (LAYERS + 1, CH), jnp.float32), 0.1, 1.9),
    }


dilation_steps = (1, 2, 4, 8)

def norm_act(stream, scale_gain):
    centre = lax.optimization_barrier(jnp.mean(stream, axis=-1, keepdims=True))
    spread = lax.optimization_barrier(jnp.mean((stream - centre) * (stream - centre), axis=-1, keepdims=True))
    normed = (stream - centre) * lax.rsqrt(spread + 1e-05) * scale_gain
    return jax.nn.gelu(normed).astype(jnp.bfloat16)

def dilated(activated, kernel, dilation):
    output = lax.conv_general_dilated(activated[None], kernel, (1, 1), ((dilation, dilation), (dilation, dilation)), rhs_dilation=(dilation, dilation), dimension_numbers=('NHWC', 'HWIO', 'NHWC'), preferred_element_type=jnp.float32)
    return output[0].astype(jnp.float32)

def reference(features, inner_weights, far_weights, gains):
    stream = features.astype(jnp.float32)
    for layer in range(LAYERS):
        dilation = dilation_steps[layer]
        stream = stream + dilated(norm_act(stream, gains[layer]), inner_weights[layer], dilation)
    stream = stream + dilated(norm_act(stream, gains[LAYERS]), far_weights, FAR)
    return stream
```

```python
import functools

import jax
import jax.numpy as jnp
from jax import lax
from jax.experimental import pallas as pl
from jax.experimental.pallas import tpu as pltpu
from jax.sharding import PartitionSpec as P

MESH = pl.DeviceIdType.MESH
CH = 384
HOP = 4
ROWS, COLS = 16, 64
WIDE = 80
R = 4


def norm_act(stream, gain, mask):
    centre = jnp.mean(stream, axis=-1, keepdims=True)
    moved = stream - centre
    spread = jnp.mean(moved * moved, axis=-1, keepdims=True)
    scale = lax.rsqrt(spread + 1e-05)
    if mask is not None:
        scale = scale * mask
    return jax.nn.gelu(moved * scale * gain).astype(jnp.bfloat16)


def dot(a, b):
    return jnp.dot(a, b, preferred_element_type=jnp.float32)


def loop(n, body):
    def step(i, carry):
        body(i)
        return carry

    lax.fori_loop(0, n, step, 0)


def kernel(
    nrow, ncol,
    feat, inner, far, gains, out,
    fx, hl, hr, u0, u1, u2, u3, s, w, wf,
    edge, edge_out, edge_in, fa, fr, fp, fq,
    in_sem, w_sem, o_sem,
    e0_s, e0_r, e2_s, e2_r, e3_s, e3_r, ed_s, ed_r, fa_s, fa_r, fp_s, fp_r,
):
    r, c = lax.axis_index("row"), lax.axis_index("col")

    def there(dr, dc):
        return (r + dr >= 0) & (r + dr < nrow) & (c + dc >= 0) & (c + dc < ncol)

    def remote(src, dst, ss, rs, dr, dc):
        return pltpu.make_async_remote_copy(
            src_ref=src, dst_ref=dst, send_sem=ss, recv_sem=rs,
            device_id=(r + dr, c + dc), device_id_type=MESH,
        )

    def send(src, dst, ss, rs, dr, dc):
        @pl.when(there(dr, dc))
        def _():
            remote(src, dst, ss, rs, dr, dc).start()

    def sent(src, dst, ss, rs, dr, dc):
        @pl.when(there(dr, dc))
        def _():
            remote(src, dst, ss, rs, dr, dc).wait_send()

    def received(dst, ss, rs, dr, dc):
        @pl.when(there(dr, dc))
        def _():
            remote(dst, dst, ss, rs, dr, dc).wait_recv()

    own_copy = pltpu.make_async_copy(feat, fx.at[pl.ds(3, ROWS), pl.ds(0, COLS)], in_sem)
    own_copy.start()

    def weights(l):
        for b in range(3):
            pltpu.make_async_copy(
                inner.at[l, :, b], w.at[l, :, :, pl.ds(b * CH, CH)], w_sem.at[l]
            ).start()

    weights(0)

    greet = [(dr, dc) for dr in (-1, 0, 1) for dc in (-1, 0, 1) if dr or dc] + [(HOP, 0), (-HOP, 0)]
    barrier = pltpu.get_barrier_semaphore()
    for dr, dc in greet:
        @pl.when(there(dr, dc))
        def _():
            pl.semaphore_signal(barrier, inc=1, device_id=(r + dr, c + dc), device_id_type=MESH)


    @pl.when(r == 0)
    def _():
        fx[0:3] = jnp.zeros((3, WIDE, CH), fx.dtype)
        hl[0:3] = jnp.zeros((3, 16, CH), hl.dtype)
        hr[0:3] = jnp.zeros((3, 16, CH), hr.dtype)
        u2[0:4] = jnp.zeros((4, WIDE, CH), u2.dtype)
        u3[0:8] = jnp.zeros((8, COLS, CH), u3.dtype)

    @pl.when(r == nrow - 1)
    def _():
        fx[19:22] = jnp.zeros((3, WIDE, CH), fx.dtype)
        hl[19:22] = jnp.zeros((3, 16, CH), hl.dtype)
        hr[19:22] = jnp.zeros((3, 16, CH), hr.dtype)
        u2[20:24] = jnp.zeros((4, WIDE, CH), u2.dtype)
        u3[24:32] = jnp.zeros((8, COLS, CH), u3.dtype)

    tile_zero = jnp.zeros((R, COLS, CH), jnp.bfloat16)

    @pl.when(c == 0)
    def _():
        hl[...] = jnp.zeros(hl.shape, hl.dtype)
        for k in range(4):
            edge_in[k, 0] = jnp.zeros((R * 8, CH), edge_in.dtype)
            (fr if k % 2 == 0 else fq)[k, 0] = tile_zero

    @pl.when(c == ncol - 1)
    def _():
        hr[...] = jnp.zeros(hr.shape, hr.dtype)
        for k in range(4):
            edge_in[k, 1] = jnp.zeros((R * 8, CH), edge_in.dtype)
            (fr if k % 2 == 0 else fq)[k, 1] = tile_zero

    @pl.when(r < HOP)
    def _():
        for k in range(4):
            (fr if k % 2 == 1 else fq)[k, 0] = tile_zero

    @pl.when(r >= nrow - HOP)
    def _():
        for k in range(4):
            (fr if k % 2 == 1 else fq)[k, 1] = tile_zero

    pl.semaphore_wait(barrier, sum(jnp.where(there(dr, dc), 1, 0) for dr, dc in greet))

    low, high, whole = pl.ds(0, 3), pl.ds(13, 3), pl.ds(0, ROWS)
    left16, right16 = pl.ds(0, 16), pl.ds(COLS - 16, 16)
    top, mid, bottom = pl.ds(0, 3), pl.ds(3, ROWS), pl.ds(19, 3)
    first = [
        (feat.at[low], fx.at[bottom, pl.ds(0, COLS)], -1, 0),
        (feat.at[high], fx.at[top, pl.ds(0, COLS)], 1, 0),
        (feat.at[low, left16], hr.at[bottom], -1, -1),
        (feat.at[low, right16], hl.at[bottom], -1, 1),
        (feat.at[high, left16], hr.at[top], 1, -1),
        (feat.at[high, right16], hl.at[top], 1, 1),
        (feat.at[whole, left16], hr.at[mid], 0, -1),
        (feat.at[whole, right16], hl.at[mid], 0, 1),
    ]
    for k, (src, dst, dr, dc) in enumerate(first):
        send(src, dst, e0_s.at[k], e0_r.at[k], dr, dc)

    def first_received(k):
        _, dst, dr, dc = first[k]
        received(dst, e0_s.at[k], e0_r.at[k], -dr, -dc)

    for l in range(1, 4):
        weights(l)
    for t in range(3):
        pltpu.make_async_copy(far.at[t], wf.at[0, :, :, pl.ds(t * CH, CH)], w_sem.at[4]).start()
        pltpu.make_async_copy(far.at[:, t], wf.at[1, :, :, pl.ds(t * CH, CH)], w_sem.at[5]).start()

    def weights_here(l):
        ref = w.at[l] if l < 4 else wf.at[l - 4]
        pltpu.make_async_copy(ref, ref, w_sem.at[l]).wait()

    def gain(l):
        return gains[l : l + 1, :][None]

    def mask(row, n):
        rows = row + lax.broadcasted_iota(jnp.int32, (n, WIDE, 1), 0)
        cols = lax.broadcasted_iota(jnp.int32, (n, WIDE, 1), 1)
        row_from = jnp.where(r == 0, 0, -8)
        row_to = jnp.where(r == nrow - 1, ROWS, ROWS + 8)
        col_from = jnp.where(c == ncol - 1, COLS + 8, COLS)
        col_to = jnp.where(c == 0, COLS + 8, WIDE)
        inside = (rows >= row_from) & (rows < row_to)
        inside = inside & ((cols < COLS) | ((cols >= col_from) & (cols < col_to)))
        return jnp.where(inside, 1.0, 0.0).astype(jnp.float32)

    def first_act(at, n):
        right = hr[pl.ds(at, n)].astype(jnp.float32)[:, :8]
        left = hl[pl.ds(at, n)].astype(jnp.float32)[:, 8:]
        halo = jnp.concatenate([right, left], axis=1)
        fx[pl.ds(at, n), COLS:] = halo.astype(jnp.bfloat16)
        value = jnp.concatenate([fx[pl.ds(at, n), :COLS].astype(jnp.float32), halo], axis=1)
        u0[pl.ds(at, n)] = norm_act(value, gain(0), None)

    def conv(u, at, d, l):
        left_side = jnp.concatenate(
            [u[pl.ds(at + a * d, R)].reshape(R * WIDE, CH) for a in range(3)], axis=-1
        )
        z = dot(left_side, w[l].reshape(3 * CH, 3 * CH))
        parts = [z[:, b * CH : (b + 1) * CH].reshape(R, WIDE, CH) for b in range(3)]
        return pltpu.roll(parts[0], d, 1) + parts[1] + pltpu.roll(parts[2], WIDE - d, 1)

    def layer0(row):
        new = fx[pl.ds(row + 3, R)].astype(jnp.float32) + conv(u0, row + 2, 1, 0)
        s[pl.ds(row + 2, R)] = new
        u1[pl.ds(row + 2, R)] = norm_act(new, gain(1), mask(row, R))

    def layer1(row):
        new = s[pl.ds(row + 2, R)] + conv(u1, row, 2, 1)
        s[pl.ds(row + 2, R)] = new
        u2[pl.ds(row + 4, R)] = norm_act(new, gain(2), mask(row, R))

    def layer2(row):
        new = s[pl.ds(row + 2, R), :COLS] + conv(u2, row, 4, 2)[:, :COLS]
        s[pl.ds(row + 2, R), :COLS] = new
        u3[pl.ds(row + 8, R)] = norm_act(new, gain(3), None)

    own_copy.wait()
    first_received(6)
    first_received(7)
    loop(4, lambda i: first_act(3 + R * i, R))
    weights_here(0)
    loop(3, lambda i: layer0(2 + R * i))
    for k in range(6):
        first_received(k)
    loop(2, lambda i: first_act(19 * i, 3))
    loop(2, lambda i: layer0(-2 + 16 * i))
    weights_here(1)
    loop(2, lambda i: layer1(12 * i))
    second = [
        (u2.at[pl.ds(4, 4)], u2.at[pl.ds(20, 4)], -1, 0),
        (u2.at[pl.ds(16, 4)], u2.at[pl.ds(0, 4)], 1, 0),
    ]
    for k, (src, dst, dr, dc) in enumerate(second):
        send(src, dst, e2_s.at[k], e2_r.at[k], dr, dc)
    loop(2, lambda i: layer1(4 + R * i))
    weights_here(2)
    loop(2, lambda i: layer2(4 + R * i))
    third = [
        (u3.at[pl.ds(16, 4)], u3.at[pl.ds(0, 4)], 1, 0),
        (u3.at[pl.ds(12, 4)], u3.at[pl.ds(28, 4)], -1, 0),
        (u3.at[pl.ds(20, 4)], u3.at[pl.ds(4, 4)], 1, 0),
        (u3.at[pl.ds(8, 4)], u3.at[pl.ds(24, 4)], -1, 0),
    ]
    for k in (0, 1):
        src, dst, dr, dc = third[k]
        send(src, dst, e3_s.at[k], e3_r.at[k], dr, dc)
    for k, (src, dst, dr, dc) in enumerate(second):
        received(dst, e2_s.at[k], e2_r.at[k], -dr, -dc)
    loop(2, lambda i: layer2(12 * i))
    for k in (2, 3):
        src, dst, dr, dc = third[k]
        send(src, dst, e3_s.at[k], e3_r.at[k], dr, dc)

    def spread_cols(z):
        z = [z[:, b * CH : (b + 1) * CH].reshape(R, COLS, CH) for b in range(3)]
        none = jnp.zeros((R, 8, CH), jnp.float32)
        here = (
            jnp.concatenate([none, z[0][:, : COLS - 8]], axis=1)
            + z[1]
            + jnp.concatenate([z[2][:, 8:], none], axis=1)
        )
        return here, z[0][:, COLS - 8 :], z[2][:, :8]

    def add(row, value):
        s[pl.ds(row + 2, R), :COLS] = s[pl.ds(row + 2, R), :COLS] + value

    def layer3_own(i):
        row = R * i
        low_row = lax.rem(row, 8)
        left_side = jnp.concatenate(
            [u3[pl.ds(8 + low_row + 8 * a, R)].reshape(R * COLS, CH) for a in range(2)], axis=-1
        )
        z = dot(left_side, w[3, pl.ds(1 - row // 8, 2)].reshape(2 * CH, 3 * CH))
        here, to_right, to_left = spread_cols(z)
        add(row, here)
        edge[i, 0] = to_right
        edge[i, 1] = to_left

    def row_of(k):
        even, late = 1 - lax.rem(k, 2), k // 2
        return even * 4 * late + (1 - even) * (12 - 4 * late)

    def layer3_halo(k):
        odd = lax.rem(k, 2)
        row = row_of(k)
        at = row + 16 * odd
        place = u3.at[pl.ds(at, R)]

        @pl.when(odd == 0)
        def _():
            received(place, e3_s.at[k], e3_r.at[k], -1, 0)

        @pl.when(odd == 1)
        def _():
            received(place, e3_s.at[k], e3_r.at[k], 1, 0)

        z = dot(u3[pl.ds(at, R)].reshape(R * COLS, CH), w[3, 2 * odd])
        here, to_right, to_left = spread_cols(z)
        add(row, here)
        i = row // R
        edge_out[k, 0] = (edge[i, 0] + to_right).reshape(R * 8, CH).astype(jnp.bfloat16)
        edge_out[k, 1] = (edge[i, 1] + to_left).reshape(R * 8, CH).astype(jnp.bfloat16)
        send(edge_out.at[k, 0], edge_in.at[k, 0], ed_s.at[k, 0], ed_r.at[k, 0], 0, 1)
        send(edge_out.at[k, 1], edge_in.at[k, 1], ed_s.at[k, 1], ed_r.at[k, 1], 0, -1)

    def move(k, first_axis, action, buf_out, buf_in, ss, rs):
        for parity in range(2):
            dr, dc = (0, 1) if (parity == 0) == first_axis else (HOP, 0)

            @pl.when(lax.rem(k, 2) == parity)
            def _():
                for side, sign in ((0, 1), (1, -1)):
                    if action == "received":
                        received(buf_in.at[k, side], ss.at[k, side], rs.at[k, side], -sign * dr, -sign * dc)
                    else:
                        fn = send if action == "send" else sent
                        src = buf_out.at[k] if first_axis else buf_out.at[k, side]
                        fn(src, buf_in.at[k, side], ss.at[k, side], rs.at[k, side], sign * dr, sign * dc)

    def layer3_end(k):
        row = row_of(k)
        received(edge_in.at[k, 0], ed_s.at[k, 0], ed_r.at[k, 0], 0, -1)
        received(edge_in.at[k, 1], ed_s.at[k, 1], ed_r.at[k, 1], 0, 1)
        old = s[pl.ds(row + 2, R), :COLS]
        from_left = edge_in[k, 0].astype(jnp.float32).reshape(R, 8, CH)
        from_right = edge_in[k, 1].astype(jnp.float32).reshape(R, 8, CH)
        new = jnp.concatenate(
            [old[:, :8] + from_left, old[:, 8 : COLS - 8], old[:, COLS - 8 :] + from_right], axis=1
        )
        s[pl.ds(row + 2, R), :COLS] = new
        fa[k] = norm_act(new, gain(4), None)
        move(k, True, "send", fa, fr, fa_s, fa_r)

    weights_here(3)
    loop(4, layer3_own)
    weights_here(4)
    weights_here(5)

    def layer3_pair(g):
        loop(2, lambda j: layer3_halo(2 * g + j))
        loop(2, lambda j: layer3_end(2 * g + j))

    loop(2, layer3_pair)

    def far_step(k):
        row = row_of(k)
        move(k, True, "received", fa, fr, fa_s, fa_r)
        left_side = jnp.concatenate(
            [v.reshape(R * COLS, CH) for v in (fr[k, 0], fa[k], fr[k, 1])], axis=-1
        )
        z = dot(left_side, wf[lax.rem(k, 2)].reshape(3 * CH, 3 * CH))
        fp[k, 0] = z[:, :CH].astype(jnp.bfloat16).reshape(R, COLS, CH)
        fp[k, 1] = z[:, 2 * CH :].astype(jnp.bfloat16).reshape(R, COLS, CH)
        move(k, False, "send", fp, fq, fp_s, fp_r)
        add(row, z[:, CH : 2 * CH].reshape(R, COLS, CH))

    loop(4, far_step)

    def out_copy(k):
        row = row_of(k)
        return pltpu.make_async_copy(s.at[pl.ds(row + 2, R), pl.ds(0, COLS)], out.at[pl.ds(row, R)], o_sem.at[k])

    def far_end(k):
        move(k, False, "received", fp, fq, fp_s, fp_r)
        add(row_of(k), fq[k, 0].astype(jnp.float32) + fq[k, 1].astype(jnp.float32))
        out_copy(k).start()

    loop(4, far_end)

    for k, (src, dst, dr, dc) in enumerate(first):
        sent(src, dst, e0_s.at[k], e0_r.at[k], dr, dc)
    for k, (src, dst, dr, dc) in enumerate(second):
        sent(src, dst, e2_s.at[k], e2_r.at[k], dr, dc)
    for k, (src, dst, dr, dc) in enumerate(third):
        sent(src, dst, e3_s.at[k], e3_r.at[k], dr, dc)

    def all_sent(k):
        sent(edge_out.at[k, 0], edge_in.at[k, 0], ed_s.at[k, 0], ed_r.at[k, 0], 0, 1)
        sent(edge_out.at[k, 1], edge_in.at[k, 1], ed_s.at[k, 1], ed_r.at[k, 1], 0, -1)
        move(k, True, "sent", fa, fr, fa_s, fa_r)
        move(k, False, "sent", fp, fq, fp_s, fp_r)
        out_copy(k).wait()

    loop(4, all_sent)


def local(nrow, ncol, features, inner_weights, far_weights, gains):
    bf16, f32 = jnp.bfloat16, jnp.float32
    dma = pltpu.SemaphoreType.DMA
    hbm = pl.BlockSpec(memory_space=pl.ANY)
    return pl.pallas_call(
        functools.partial(kernel, nrow, ncol),
        out_shape=jax.ShapeDtypeStruct(features.shape, f32),
        in_specs=[hbm, hbm, hbm, pl.BlockSpec(memory_space=pltpu.VMEM)],
        out_specs=hbm,
        scratch_shapes=[
            pltpu.VMEM((ROWS + 6, WIDE, CH), bf16),
            pltpu.VMEM((ROWS + 6, 16, CH), bf16),
            pltpu.VMEM((ROWS + 6, 16, CH), bf16),
            pltpu.VMEM((ROWS + 6, WIDE, CH), bf16),
            pltpu.VMEM((ROWS + 4, WIDE, CH), bf16),
            pltpu.VMEM((ROWS + 8, WIDE, CH), bf16),
            pltpu.VMEM((ROWS + 16, COLS, CH), bf16),
            pltpu.VMEM((ROWS + 4, WIDE, CH), f32),
            pltpu.VMEM((4, 3, CH, 3 * CH), bf16),
            pltpu.VMEM((2, 3, CH, 3 * CH), bf16),
            pltpu.VMEM((4, 2, R, 8, CH), f32),
            pltpu.VMEM((4, 2, R * 8, CH), bf16),
            pltpu.VMEM((4, 2, R * 8, CH), bf16),
            pltpu.VMEM((4, R, COLS, CH), bf16),
            pltpu.VMEM((4, 2, R, COLS, CH), bf16),
            pltpu.VMEM((4, 2, R, COLS, CH), bf16),
            pltpu.VMEM((4, 2, R, COLS, CH), bf16),
            dma, dma((6,)), dma((4,)),
            dma((8,)), dma((8,)), dma((2,)), dma((2,)), dma((4,)), dma((4,)),
            dma((4, 2)), dma((4, 2)), dma((4, 2)), dma((4, 2)), dma((4, 2)), dma((4, 2)),
        ],
        compiler_params=pltpu.CompilerParams(
            collective_id=0, has_side_effects=True, vmem_limit_bytes=56 * 2**20
        ),
    )(features, inner_weights, far_weights, gains)


def solution(mesh):
    return jax.shard_map(
        functools.partial(local, mesh.shape["row"], mesh.shape["col"]),
        mesh=mesh,
        in_specs=(P("row", "col", None), P(), P(), P()),
        out_specs=P("row", "col", None),
        check_vma=False,
    )
```

```python
import functools

import jax
import jax.numpy as jnp
from jax import lax
from jax.experimental import pallas as pl
from jax.experimental.pallas import tpu as pltpu
from jax.sharding import PartitionSpec as P

MESH = pl.DeviceIdType.MESH
CH = 384
HOP = 4
ROWS, COLS = 16, 64
WIDE = 80
R = 4


def norm_act(stream, gain, mask):
    centre = jnp.mean(stream, axis=-1, keepdims=True)
    moved = stream - centre
    spread = jnp.mean(moved * moved, axis=-1, keepdims=True)
    scale = lax.rsqrt(spread + 1e-05)
    if mask is not None:
        scale = scale * mask
    return jax.nn.gelu(moved * scale * gain).astype(jnp.bfloat16)


def dot(a, b):
    return jnp.dot(a, b, preferred_element_type=jnp.float32)


def row8(row):
    return row * 8 if isinstance(row, int) else pl.multiple_of(row * 8, 32)


def unrolled(n, body):
    for i in range(n):
        body(i)


def loop(n, body):
    def step(i, carry):
        body(i)
        return carry

    lax.fori_loop(0, n, step, 0)


def kernel(
    nrow, ncol,
    feat, inner, far, gains, out,
    fx, pk, hb, u0, u1, u2, u3, pk3, hb3, s, zh, w, wf,
    fa, fr, fp, fq,
    in_sem, w_sem, o_sem,
    e0_s, e0_r, e2_s, e2_r, e3_s, e3_r, x3_s, x3_r, d3_s, d3_r, fa_s, fa_r, fp_s, fp_r,
):
    r, c = lax.axis_index("row"), lax.axis_index("col")

    def there(dr, dc):
        return (r + dr >= 0) & (r + dr < nrow) & (c + dc >= 0) & (c + dc < ncol)

    def remote(src, dst, ss, rs, dr, dc):
        return pltpu.make_async_remote_copy(
            src_ref=src, dst_ref=dst, send_sem=ss, recv_sem=rs,
            device_id=(r + dr, c + dc), device_id_type=MESH,
        )

    def send(src, dst, ss, rs, dr, dc):
        @pl.when(there(dr, dc))
        def _():
            remote(src, dst, ss, rs, dr, dc).start()

    def sent(src, dst, ss, rs, dr, dc):
        @pl.when(there(dr, dc))
        def _():
            remote(src, dst, ss, rs, dr, dc).wait_send()

    def received(dst, ss, rs, dr, dc):
        @pl.when(there(dr, dc))
        def _():
            remote(dst, dst, ss, rs, dr, dc).wait_recv()

    own_copy = pltpu.make_async_copy(feat, fx.at[pl.ds(4, ROWS), pl.ds(0, COLS)], in_sem)
    own_copy.start()

    def weights(l):
        for b in range(3):
            pltpu.make_async_copy(
                inner.at[l, :, b], w.at[l, :, :, pl.ds(b * CH, CH)], w_sem.at[l]
            ).start()

    weights(0)

    greet = [(dr, dc) for dr in (-1, 0, 1) for dc in (-1, 0, 1) if dr or dc] + [(HOP, 0), (-HOP, 0)]
    barrier = pltpu.get_barrier_semaphore()
    for dr, dc in greet:
        @pl.when(there(dr, dc))
        def _():
            pl.semaphore_signal(barrier, inc=1, device_id=(r + dr, c + dc), device_id_type=MESH)


    @pl.when(r == 0)
    def _():
        fx[0:4, :COLS] = jnp.zeros((4, COLS, CH), fx.dtype)
        u2[0:4] = jnp.zeros((4, WIDE, CH), u2.dtype)
        u3[0:8] = jnp.zeros((8, COLS, CH), u3.dtype)
        for side in range(2):
            hb[side, 0:32] = jnp.zeros((32, CH), hb.dtype)
            hb3[side, 0:64] = jnp.zeros((64, CH), hb3.dtype)

    @pl.when(r == nrow - 1)
    def _():
        fx[20:24, :COLS] = jnp.zeros((4, COLS, CH), fx.dtype)
        u2[20:24] = jnp.zeros((4, WIDE, CH), u2.dtype)
        u3[24:32] = jnp.zeros((8, COLS, CH), u3.dtype)
        for side in range(2):
            hb[side, 160:192] = jnp.zeros((32, CH), hb.dtype)
            hb3[side, 192:256] = jnp.zeros((64, CH), hb3.dtype)

    tile_zero = jnp.zeros((R, COLS, CH), jnp.bfloat16)

    @pl.when(c == 0)
    def _():
        hb[1] = jnp.zeros((192, CH), hb.dtype)
        hb3[1] = jnp.zeros((256, CH), hb3.dtype)
        for k in range(4):
            (fr if k % 2 == 0 else fq)[k, 0] = tile_zero

    @pl.when(c == ncol - 1)
    def _():
        hb[0] = jnp.zeros((192, CH), hb.dtype)
        hb3[0] = jnp.zeros((256, CH), hb3.dtype)
        for k in range(4):
            (fr if k % 2 == 0 else fq)[k, 1] = tile_zero

    @pl.when(r < HOP)
    def _():
        for k in range(4):
            (fr if k % 2 == 1 else fq)[k, 0] = tile_zero

    @pl.when(r >= nrow - HOP)
    def _():
        for k in range(4):
            (fr if k % 2 == 1 else fq)[k, 1] = tile_zero

    def gain(l):
        return gains[l : l + 1, :][None]

    def flat(value):
        n = value.shape[0]
        return value.reshape(n * 8, CH).astype(jnp.bfloat16)

    def unflat(ref, side, row, n):
        at = pl.multiple_of(row * 8, 16)
        return ref[side, pl.ds(at, n * 8)].astype(jnp.float32).reshape(n, 8, CH)

    def own_act(i):
        row = R * i
        value = fx[pl.ds(row + 4, R), :COLS].astype(jnp.float32)
        at = pl.ds(row8(row), R * 8)
        pk[0, at] = flat(value[:, :8])
        pk[1, at] = flat(value[:, COLS - 8 :])
        u0[pl.ds(row + 4, R), :COLS] = norm_act(value, gain(0), None)

    own_copy.wait()
    loop(4, own_act)
    pl.semaphore_wait(barrier, sum(jnp.where(there(dr, dc), 1, 0) for dr, dc in greet))

    own = pl.ds(0, COLS)
    top, mid, bottom = pl.ds(0, 32), pl.ds(32, ROWS * 8), pl.ds(160, 32)
    head, tail = pl.ds(0, 32), pl.ds(96, 32)
    first = [
        (feat.at[pl.ds(0, 3)], fx.at[pl.ds(20, 3), own], -1, 0),
        (feat.at[pl.ds(13, 3)], fx.at[pl.ds(1, 3), own], 1, 0),
        (pk.at[0, head], hb.at[0, bottom], -1, -1),
        (pk.at[1, head], hb.at[1, bottom], -1, 1),
        (pk.at[0, tail], hb.at[0, top], 1, -1),
        (pk.at[1, tail], hb.at[1, top], 1, 1),
        (pk.at[0], hb.at[0, mid], 0, -1),
        (pk.at[1], hb.at[1, mid], 0, 1),
    ]
    for k, (src, dst, dr, dc) in enumerate(first):
        send(src, dst, e0_s.at[k], e0_r.at[k], dr, dc)

    def first_received(k):
        _, dst, dr, dc = first[k]
        received(dst, e0_s.at[k], e0_r.at[k], -dr, -dc)

    for l in range(1, 4):
        weights(l)
    for t in range(3):
        pltpu.make_async_copy(far.at[t], wf.at[0, :, :, pl.ds(t * CH, CH)], w_sem.at[4]).start()
        pltpu.make_async_copy(far.at[:, t], wf.at[1, :, :, pl.ds(t * CH, CH)], w_sem.at[5]).start()

    def weights_here(l):
        ref = w.at[l] if l < 4 else wf.at[l - 4]
        pltpu.make_async_copy(ref, ref, w_sem.at[l]).wait()

    def mask(row, n):
        rows = row + lax.broadcasted_iota(jnp.int32, (n, WIDE, 1), 0)
        cols = lax.broadcasted_iota(jnp.int32, (n, WIDE, 1), 1)
        row_from = jnp.where(r == 0, 0, -8)
        row_to = jnp.where(r == nrow - 1, ROWS, ROWS + 8)
        col_from = jnp.where(c == ncol - 1, COLS + 8, COLS)
        col_to = jnp.where(c == 0, COLS + 8, WIDE)
        inside = (rows >= row_from) & (rows < row_to)
        inside = inside & ((cols < COLS) | ((cols >= col_from) & (cols < col_to)))
        return jnp.where(inside, 1.0, 0.0).astype(jnp.float32)

    def halo_cols(row, n):
        return jnp.concatenate([unflat(hb, 0, row + 4, n), unflat(hb, 1, row + 4, n)], axis=1)

    def halo_act(i):
        row = R * i
        halo = halo_cols(row, R)
        fx[pl.ds(row + 4, R), COLS:] = halo.astype(jnp.bfloat16)
        u0[pl.ds(row + 4, R), COLS:] = norm_act(halo, gain(0), None)

    def outer_act(i):
        row = 20 * i - 4
        halo = halo_cols(row, R)
        fx[pl.ds(row + 4, R), COLS:] = halo.astype(jnp.bfloat16)
        value = jnp.concatenate([fx[pl.ds(row + 4, R), :COLS].astype(jnp.float32), halo], axis=1)
        u0[pl.ds(row + 4, R)] = norm_act(value, gain(0), None)

    def shifted(parts, d):
        return pltpu.roll(parts[0], d, 1) + parts[1] + pltpu.roll(parts[2], WIDE - d, 1)

    def layer0_own(row):
        left_side = jnp.concatenate(
            [u0[pl.ds(row + 3 + a, R), :COLS].reshape(R * COLS, CH) for a in range(3)], axis=-1
        )
        z = dot(left_side, w[0].reshape(3 * CH, 3 * CH))
        none = jnp.zeros((R, WIDE - COLS, CH), jnp.float32)
        parts = [
            jnp.concatenate([z[:, b * CH : (b + 1) * CH].reshape(R, COLS, CH), none], axis=1)
            for b in range(3)
        ]
        s[pl.ds(row + 2, R)] = shifted(parts, 1)

    def layer0_halo_dot():
        n = 3 * R
        left_side = jnp.concatenate(
            [u0[pl.ds(5 + a, n), COLS:].reshape(n * 16, CH) for a in range(3)], axis=-1
        )
        zh[...] = dot(left_side, w[0].reshape(3 * CH, 3 * CH)).reshape(n, 16, 3 * CH)

    def layer0_halo(i):
        row = 2 + R * i
        z = zh[pl.ds(R * i, R)]
        none = jnp.zeros((R, COLS, CH), jnp.float32)
        parts = [jnp.concatenate([none, z[:, :, b * CH : (b + 1) * CH]], axis=1) for b in range(3)]
        new = fx[pl.ds(row + 4, R)].astype(jnp.float32) + s[pl.ds(row + 2, R)] + shifted(parts, 1)
        s[pl.ds(row + 2, R)] = new
        u1[pl.ds(row + 2, R)] = norm_act(new, gain(1), mask(row, R))

    def conv(u, at, d, l):
        left_side = jnp.concatenate(
            [u[pl.ds(at + a * d, R)].reshape(R * WIDE, CH) for a in range(3)], axis=-1
        )
        z = dot(left_side, w[l].reshape(3 * CH, 3 * CH))
        parts = [z[:, b * CH : (b + 1) * CH].reshape(R, WIDE, CH) for b in range(3)]
        return shifted(parts, d)

    def layer0(row):
        new = fx[pl.ds(row + 4, R)].astype(jnp.float32) + conv(u0, row + 3, 1, 0)
        s[pl.ds(row + 2, R)] = new
        u1[pl.ds(row + 2, R)] = norm_act(new, gain(1), mask(row, R))

    def layer1(row):
        new = s[pl.ds(row + 2, R)] + conv(u1, row, 2, 1)
        s[pl.ds(row + 2, R)] = new
        u2[pl.ds(row + 4, R)] = norm_act(new, gain(2), mask(row, R))

    def layer2(row):
        new = s[pl.ds(row + 2, R), :COLS] + conv(u2, row, 4, 2)[:, :COLS]
        s[pl.ds(row + 2, R), :COLS] = new
        act = norm_act(new, gain(3), None)
        u3[pl.ds(row + 8, R)] = act
        at = pl.ds(row8(row), R * 8)
        act = act.astype(jnp.float32)
        pk3[0, at] = flat(act[:, :8])
        pk3[1, at] = flat(act[:, COLS - 8 :])

    weights_here(0)
    loop(3, lambda i: layer0_own(2 + R * i))
    first_received(6)
    first_received(7)
    loop(4, halo_act)
    layer0_halo_dot()
    loop(3, layer0_halo)
    for k in range(6):
        first_received(k)
    loop(2, outer_act)
    unrolled(2, lambda i: layer0(-2 + 16 * i))
    weights_here(1)
    unrolled(2, lambda i: layer1(12 * i))
    second = [
        (u2.at[pl.ds(4, 4)], u2.at[pl.ds(20, 4)], -1, 0),
        (u2.at[pl.ds(16, 4)], u2.at[pl.ds(0, 4)], 1, 0),
    ]
    for k, (src, dst, dr, dc) in enumerate(second):
        send(src, dst, e2_s.at[k], e2_r.at[k], dr, dc)
    unrolled(2, lambda i: layer1(4 + R * i))
    weights_here(2)
    unrolled(2, lambda i: layer2(4 + R * i))
    third = [
        (u3.at[pl.ds(16, 4)], u3.at[pl.ds(0, 4)], 1, 0),
        (u3.at[pl.ds(12, 4)], u3.at[pl.ds(28, 4)], -1, 0),
        (u3.at[pl.ds(20, 4)], u3.at[pl.ds(4, 4)], 1, 0),
        (u3.at[pl.ds(8, 4)], u3.at[pl.ds(24, 4)], -1, 0),
    ]
    third_from = (8, 4, 12, 0)
    third_to = (-8, 20, -4, 16)

    def columns(k):
        for side, dc in ((0, -1), (1, 1)):
            src = pk3.at[side, pl.ds(third_from[k] * 8, 32)]
            here = hb3.at[side, pl.ds((third_from[k] + 8) * 8, 32)]
            corner = hb3.at[side, pl.ds((third_to[k] + 8) * 8, 32)]
            yield src, here, x3_s.at[k, side], x3_r.at[k, side], 0, dc
            yield src, corner, d3_s.at[k, side], d3_r.at[k, side], third[k][2], dc

    def third_send(k):
        src, dst, dr, dc = third[k]
        send(src, dst, e3_s.at[k], e3_r.at[k], dr, dc)
        for args in columns(k):
            send(*args)

    third_send(0)
    third_send(1)
    for k, (src, dst, dr, dc) in enumerate(second):
        received(dst, e2_s.at[k], e2_r.at[k], -dr, -dc)
    unrolled(2, lambda i: layer2(12 * i))
    third_send(2)
    third_send(3)

    def spread_cols(z):
        z = [z[:, b * CH : (b + 1) * CH].reshape(R, COLS, CH) for b in range(3)]
        none = jnp.zeros((R, 8, CH), jnp.float32)
        return (
            jnp.concatenate([none, z[0][:, : COLS - 8]], axis=1)
            + z[1]
            + jnp.concatenate([z[2][:, 8:], none], axis=1)
        )

    def add(row, value):
        s[pl.ds(row + 2, R), :COLS] = s[pl.ds(row + 2, R), :COLS] + value

    def layer3_own(i):
        row = R * i
        low_row = lax.rem(row, 8)
        left_side = jnp.concatenate(
            [u3[pl.ds(8 + low_row + 8 * a, R)].reshape(R * COLS, CH) for a in range(2)], axis=-1
        )
        z = dot(left_side, w[3, pl.ds(1 - row // 8, 2)].reshape(2 * CH, 3 * CH))
        add(row, spread_cols(z))

    def row_of(k):
        even, late = 1 - lax.rem(k, 2), k // 2
        return even * 4 * late + (1 - even) * (12 - 4 * late)

    def move(k, first_axis, action, buf_out, buf_in, ss, rs):
        for parity in range(2):
            dr, dc = (0, 1) if (parity == 0) == first_axis else (HOP, 0)

            @pl.when(lax.rem(k, 2) == parity)
            def _():
                for side, sign in ((0, 1), (1, -1)):
                    if action == "received":
                        received(buf_in.at[k, side], ss.at[k, side], rs.at[k, side], -sign * dr, -sign * dc)
                    else:
                        fn = send if action == "send" else sent
                        src = buf_out.at[k] if first_axis else buf_out.at[k, side]
                        fn(src, buf_in.at[k, side], ss.at[k, side], rs.at[k, side], sign * dr, sign * dc)

    def column_taps(side, rows):
        left_side = jnp.concatenate(
            [
                jnp.concatenate(
                    [hb3[side, pl.ds(pl.multiple_of((row + 8 * a) * 8, 32), R * 8)] for a in range(3)],
                    axis=-1,
                )
                for row in rows
            ],
            axis=0,
        )
        b = 2 if side == 0 else 0
        return dot(left_side, w[3, :, :, b * CH : (b + 1) * CH].reshape(3 * CH, CH))

    def layer3_pair(g):
        rows = (R * g, 12 - R * g)
        from_right = column_taps(0, rows)
        from_left = column_taps(1, rows)
        for odd in range(2):
            k, row = 2 * g + odd, rows[odd]
            z = dot(u3[pl.ds(row + 16 * odd, R)].reshape(R * COLS, CH), w[3, 2 * odd])
            new = s[pl.ds(row + 2, R), :COLS] + spread_cols(z)
            part = slice(odd * R * 8, (odd + 1) * R * 8)
            new = jnp.concatenate(
                [
                    new[:, :8] + from_left[part].reshape(R, 8, CH),
                    new[:, 8 : COLS - 8],
                    new[:, COLS - 8 :] + from_right[part].reshape(R, 8, CH),
                ],
                axis=1,
            )
            s[pl.ds(row + 2, R), :COLS] = new
            fa[k] = norm_act(new, gain(4), None)

    def third_received(k):
        src, dst, dr, dc = third[k]
        received(dst, e3_s.at[k], e3_r.at[k], -dr, -dc)
        for (_, dst, ss, rs, dr, dc) in list(columns(k))[1::2]:
            received(dst, ss, rs, -dr, -dc)

    weights_here(3)
    loop(4, layer3_own)
    weights_here(4)
    weights_here(5)

    for k in range(4):
        for (_, dst, ss, rs, dr, dc) in list(columns(k))[0::2]:
            received(dst, ss, rs, -dr, -dc)

    def far_send(k):
        move(k, True, "send", fa, fr, fa_s, fa_r)

    def far_sent(k):
        move(k, True, "sent", fa, fr, fa_s, fa_r)

    def layer3_turn(g):
        for turn in range(2):
            @pl.when(g == turn)
            def _():
                third_received(2 * turn)
                third_received(2 * turn + 1)

        layer3_pair(g)

    loop(2, layer3_turn)
    for k in (0, 1):
        far_send(k)
    for k in (0, 1):
        far_sent(k)
    for k in (2, 3):
        far_send(k)

    def far_step(k):
        row = row_of(k)
        move(k, True, "received", fa, fr, fa_s, fa_r)
        left_side = jnp.concatenate(
            [v.reshape(R * COLS, CH) for v in (fr[k, 0], fa[k], fr[k, 1])], axis=-1
        )
        z = dot(left_side, wf[lax.rem(k, 2)].reshape(3 * CH, 3 * CH))
        fp[k, 0] = z[:, :CH].astype(jnp.bfloat16).reshape(R, COLS, CH)
        fp[k, 1] = z[:, 2 * CH :].astype(jnp.bfloat16).reshape(R, COLS, CH)
        move(k, False, "send", fp, fq, fp_s, fp_r)
        add(row, z[:, CH : 2 * CH].reshape(R, COLS, CH))

    loop(4, far_step)

    def out_copy(k):
        row = row_of(k)
        return pltpu.make_async_copy(s.at[pl.ds(row + 2, R), pl.ds(0, COLS)], out.at[pl.ds(row, R)], o_sem.at[k])

    def far_end(k):
        move(k, False, "received", fp, fq, fp_s, fp_r)
        add(row_of(k), fq[k, 0].astype(jnp.float32) + fq[k, 1].astype(jnp.float32))
        out_copy(k).start()

    loop(4, far_end)

    for k, (src, dst, dr, dc) in enumerate(first):
        sent(src, dst, e0_s.at[k], e0_r.at[k], dr, dc)
    for k, (src, dst, dr, dc) in enumerate(second):
        sent(src, dst, e2_s.at[k], e2_r.at[k], dr, dc)
    for k, (src, dst, dr, dc) in enumerate(third):
        sent(src, dst, e3_s.at[k], e3_r.at[k], dr, dc)
        for args in columns(k):
            sent(*args)

    def all_sent(k):
        @pl.when(k >= 2)
        def _():
            far_sent(k)

        move(k, False, "sent", fp, fq, fp_s, fp_r)
        out_copy(k).wait()

    loop(4, all_sent)


def local(nrow, ncol, features, inner_weights, far_weights, gains):
    bf16, f32 = jnp.bfloat16, jnp.float32
    dma = pltpu.SemaphoreType.DMA
    hbm = pl.BlockSpec(memory_space=pl.ANY)
    return pl.pallas_call(
        functools.partial(kernel, nrow, ncol),
        out_shape=jax.ShapeDtypeStruct(features.shape, f32),
        in_specs=[hbm, hbm, hbm, pl.BlockSpec(memory_space=pltpu.VMEM)],
        out_specs=hbm,
        scratch_shapes=[
            pltpu.VMEM((ROWS + 8, WIDE, CH), bf16),
            pltpu.VMEM((2, ROWS * 8, CH), bf16),
            pltpu.VMEM((2, (ROWS + 8) * 8, CH), bf16),
            pltpu.VMEM((ROWS + 8, WIDE, CH), bf16),
            pltpu.VMEM((ROWS + 4, WIDE, CH), bf16),
            pltpu.VMEM((ROWS + 8, WIDE, CH), bf16),
            pltpu.VMEM((ROWS + 16, COLS, CH), bf16),
            pltpu.VMEM((2, ROWS * 8, CH), bf16),
            pltpu.VMEM((2, (ROWS + 16) * 8, CH), bf16),
            pltpu.VMEM((ROWS + 4, WIDE, CH), f32),
            pltpu.VMEM((3 * R, 16, 3 * CH), f32),
            pltpu.VMEM((4, 3, CH, 3 * CH), bf16),
            pltpu.VMEM((2, 3, CH, 3 * CH), bf16),
            pltpu.VMEM((4, R, COLS, CH), bf16),
            pltpu.VMEM((4, 2, R, COLS, CH), bf16),
            pltpu.VMEM((4, 2, R, COLS, CH), bf16),
            pltpu.VMEM((4, 2, R, COLS, CH), bf16),
            dma, dma((6,)), dma((4,)),
            dma((8,)), dma((8,)), dma((2,)), dma((2,)), dma((4,)), dma((4,)),
            dma((4, 2)), dma((4, 2)), dma((4, 2)), dma((4, 2)), dma((4, 2)), dma((4, 2)), dma((4, 2)), dma((4, 2)),
        ],
        compiler_params=pltpu.CompilerParams(
            collective_id=0, has_side_effects=True, vmem_limit_bytes=50 * 2**20
        ),
    )(features, inner_weights, far_weights, gains)


def solution(mesh):
    return jax.shard_map(
        functools.partial(local, mesh.shape["row"], mesh.shape["col"]),
        mesh=mesh,
        in_specs=(P("row", "col", None), P(), P(), P()),
        out_specs=P("row", "col", None),
        check_vma=False,
    )
```

```python
import functools

import jax
import jax.numpy as jnp
from jax import lax
from jax.experimental import pallas as pl
from jax.experimental.pallas import tpu as pltpu
from jax.sharding import PartitionSpec as P

MESH = pl.DeviceIdType.MESH
CH = 384
HOP = 4
ROWS, COLS = 16, 64
WIDE = 80
R = 4


def norm_act(stream, gain, mask):
    centre = jnp.mean(stream, axis=-1, keepdims=True)
    moved = stream - centre
    spread = jnp.mean(moved * moved, axis=-1, keepdims=True)
    scale = lax.rsqrt(spread + 1e-05)
    if mask is not None:
        scale = scale * mask
    return jax.nn.gelu(moved * scale * gain).astype(jnp.bfloat16)


def dot(a, b):
    return jnp.dot(a, b, preferred_element_type=jnp.float32)


def row8(row):
    return row * 8 if isinstance(row, int) else pl.multiple_of(row * 8, 32)


def unrolled(n, body):
    for i in range(n):
        body(i)


def loop(n, body):
    def step(i, carry):
        body(i)
        return carry

    lax.fori_loop(0, n, step, 0)


def kernel(
    nrow, ncol,
    feat, inner, far, gains_in, out,
    gains, fx, pk, hb, u0, u1, u2, u3, pk3, hb3, s, zh, w, wf,
    fa, fr, fp, fq,
    in_sem, g_sem, w_sem,
    e0_s, e0_r, e2_s, e2_r, e3_s, e3_r, x3_s, x3_r, d3_s, d3_r, fa_s, fa_r, fp_s, fp_r,
):
    r, c = lax.axis_index("row"), lax.axis_index("col")

    def there(dr, dc):
        return (r + dr >= 0) & (r + dr < nrow) & (c + dc >= 0) & (c + dc < ncol)

    def remote(src, dst, ss, rs, dr, dc):
        return pltpu.make_async_remote_copy(
            src_ref=src, dst_ref=dst, send_sem=ss, recv_sem=rs,
            device_id=(r + dr, c + dc), device_id_type=MESH,
        )

    def send(src, dst, ss, rs, dr, dc):
        @pl.when(there(dr, dc))
        def _():
            remote(src, dst, ss, rs, dr, dc).start()

    def sent(src, dst, ss, rs, dr, dc):
        @pl.when(there(dr, dc))
        def _():
            remote(src, dst, ss, rs, dr, dc).wait_send()

    def received(dst, ss, rs, dr, dc):
        @pl.when(there(dr, dc))
        def _():
            remote(dst, dst, ss, rs, dr, dc).wait_recv()

    own_copy = pltpu.make_async_copy(feat, fx.at[pl.ds(4, ROWS), pl.ds(0, COLS)], in_sem)
    own_copy.start()
    gains_copy = pltpu.make_async_copy(gains_in, gains, g_sem)
    gains_copy.start()

    def weights(l):
        for b in range(3):
            pltpu.make_async_copy(
                inner.at[l, :, b], w.at[l, :, :, pl.ds(b * CH, CH)], w_sem.at[l]
            ).start()

    weights(0)

    greet = [(dr, dc) for dr in (-1, 0, 1) for dc in (-1, 0, 1) if dr or dc] + [(HOP, 0), (-HOP, 0)]
    barrier = pltpu.get_barrier_semaphore()
    for dr, dc in greet:
        @pl.when(there(dr, dc))
        def _():
            pl.semaphore_signal(barrier, inc=1, device_id=(r + dr, c + dc), device_id_type=MESH)


    @pl.when(r == 0)
    def _():
        fx[0:4, :COLS] = jnp.zeros((4, COLS, CH), fx.dtype)
        u2[0:4] = jnp.zeros((4, WIDE, CH), u2.dtype)
        u3[0:8] = jnp.zeros((8, COLS, CH), u3.dtype)
        for side in range(2):
            hb[side, 0:32] = jnp.zeros((32, CH), hb.dtype)
            hb3[side, 0:64] = jnp.zeros((64, CH), hb3.dtype)

    @pl.when(r == nrow - 1)
    def _():
        fx[20:24, :COLS] = jnp.zeros((4, COLS, CH), fx.dtype)
        u2[20:24] = jnp.zeros((4, WIDE, CH), u2.dtype)
        u3[24:32] = jnp.zeros((8, COLS, CH), u3.dtype)
        for side in range(2):
            hb[side, 160:192] = jnp.zeros((32, CH), hb.dtype)
            hb3[side, 192:256] = jnp.zeros((64, CH), hb3.dtype)

    tile_zero = jnp.zeros((R, COLS, CH), jnp.bfloat16)

    @pl.when(c == 0)
    def _():
        hb[1] = jnp.zeros((192, CH), hb.dtype)
        hb3[1] = jnp.zeros((256, CH), hb3.dtype)
        for k in range(4):
            (fr if k % 2 == 0 else fq)[k, 0] = tile_zero

    @pl.when(c == ncol - 1)
    def _():
        hb[0] = jnp.zeros((192, CH), hb.dtype)
        hb3[0] = jnp.zeros((256, CH), hb3.dtype)
        for k in range(4):
            (fr if k % 2 == 0 else fq)[k, 1] = tile_zero

    @pl.when(r < HOP)
    def _():
        for k in range(4):
            (fr if k % 2 == 1 else fq)[k, 0] = tile_zero

    @pl.when(r >= nrow - HOP)
    def _():
        for k in range(4):
            (fr if k % 2 == 1 else fq)[k, 1] = tile_zero

    def gain(l):
        return gains[l : l + 1, :][None]

    def flat(value):
        n = value.shape[0]
        return value.reshape(n * 8, CH).astype(jnp.bfloat16)

    def unflat(ref, side, row, n):
        at = pl.multiple_of(row * 8, 16)
        return ref[side, pl.ds(at, n * 8)].astype(jnp.float32).reshape(n, 8, CH)

    def own_act(i):
        row = R * i
        value = fx[pl.ds(row + 4, R), :COLS].astype(jnp.float32)
        at = pl.ds(row8(row), R * 8)
        pk[0, at] = flat(value[:, :8])
        pk[1, at] = flat(value[:, COLS - 8 :])
        u0[pl.ds(row + 4, R), :COLS] = norm_act(value, gain(0), None)

    gains_copy.wait()
    own_copy.wait()
    loop(4, own_act)
    pl.semaphore_wait(barrier, sum(jnp.where(there(dr, dc), 1, 0) for dr, dc in greet))

    own = pl.ds(0, COLS)
    top, mid, bottom = pl.ds(0, 32), pl.ds(32, ROWS * 8), pl.ds(160, 32)
    head, tail = pl.ds(0, 32), pl.ds(96, 32)
    first = [
        (feat.at[pl.ds(0, 3)], fx.at[pl.ds(20, 3), own], -1, 0),
        (feat.at[pl.ds(13, 3)], fx.at[pl.ds(1, 3), own], 1, 0),
        (pk.at[0, head], hb.at[0, bottom], -1, -1),
        (pk.at[1, head], hb.at[1, bottom], -1, 1),
        (pk.at[0, tail], hb.at[0, top], 1, -1),
        (pk.at[1, tail], hb.at[1, top], 1, 1),
        (pk.at[0], hb.at[0, mid], 0, -1),
        (pk.at[1], hb.at[1, mid], 0, 1),
    ]
    for k, (src, dst, dr, dc) in enumerate(first):
        send(src, dst, e0_s.at[k], e0_r.at[k], dr, dc)

    def first_received(k):
        _, dst, dr, dc = first[k]
        received(dst, e0_s.at[k], e0_r.at[k], -dr, -dc)

    for l in range(1, 4):
        weights(l)
    for t in range(3):
        pltpu.make_async_copy(far.at[t], wf.at[0, :, :, pl.ds(t * CH, CH)], w_sem.at[4]).start()
        pltpu.make_async_copy(far.at[:, t], wf.at[1, :, :, pl.ds(t * CH, CH)], w_sem.at[5]).start()

    def weights_here(l):
        ref = w.at[l] if l < 4 else wf.at[l - 4]
        pltpu.make_async_copy(ref, ref, w_sem.at[l]).wait()

    def mask(row, n):
        rows = row + lax.broadcasted_iota(jnp.int32, (n, WIDE, 1), 0)
        cols = lax.broadcasted_iota(jnp.int32, (n, WIDE, 1), 1)
        row_from = jnp.where(r == 0, 0, -8)
        row_to = jnp.where(r == nrow - 1, ROWS, ROWS + 8)
        col_from = jnp.where(c == ncol - 1, COLS + 8, COLS)
        col_to = jnp.where(c == 0, COLS + 8, WIDE)
        inside = (rows >= row_from) & (rows < row_to)
        inside = inside & ((cols < COLS) | ((cols >= col_from) & (cols < col_to)))
        return jnp.where(inside, 1.0, 0.0).astype(jnp.float32)

    def halo_cols(row, n):
        return jnp.concatenate([unflat(hb, 0, row + 4, n), unflat(hb, 1, row + 4, n)], axis=1)

    def halo_act(i):
        row = R * i
        halo = halo_cols(row, R)
        fx[pl.ds(row + 4, R), COLS:] = halo.astype(jnp.bfloat16)
        u0[pl.ds(row + 4, R), COLS:] = norm_act(halo, gain(0), None)

    def outer_act(i):
        row = 20 * i - 4
        halo = halo_cols(row, R)
        fx[pl.ds(row + 4, R), COLS:] = halo.astype(jnp.bfloat16)
        value = jnp.concatenate([fx[pl.ds(row + 4, R), :COLS].astype(jnp.float32), halo], axis=1)
        u0[pl.ds(row + 4, R)] = norm_act(value, gain(0), None)

    def shifted(parts, d):
        return pltpu.roll(parts[0], d, 1) + parts[1] + pltpu.roll(parts[2], WIDE - d, 1)

    def layer0_own(row):
        left_side = jnp.concatenate(
            [u0[pl.ds(row + 3 + a, R), :COLS].reshape(R * COLS, CH) for a in range(3)], axis=-1
        )
        z = dot(left_side, w[0].reshape(3 * CH, 3 * CH))
        none = jnp.zeros((R, WIDE - COLS, CH), jnp.float32)
        parts = [
            jnp.concatenate([z[:, b * CH : (b + 1) * CH].reshape(R, COLS, CH), none], axis=1)
            for b in range(3)
        ]
        s[pl.ds(row + 2, R)] = shifted(parts, 1)

    def layer0_halo_dot():
        n = 3 * R
        left_side = jnp.concatenate(
            [u0[pl.ds(5 + a, n), COLS:].reshape(n * 16, CH) for a in range(3)], axis=-1
        )
        zh[...] = dot(left_side, w[0].reshape(3 * CH, 3 * CH)).reshape(n, 16, 3 * CH)

    def layer0_halo(i):
        row = 2 + R * i
        z = zh[pl.ds(R * i, R)]
        none = jnp.zeros((R, COLS, CH), jnp.float32)
        parts = [jnp.concatenate([none, z[:, :, b * CH : (b + 1) * CH]], axis=1) for b in range(3)]
        new = fx[pl.ds(row + 4, R)].astype(jnp.float32) + s[pl.ds(row + 2, R)] + shifted(parts, 1)
        s[pl.ds(row + 2, R)] = new
        u1[pl.ds(row + 2, R)] = norm_act(new, gain(1), mask(row, R))

    def conv(u, at, d, l):
        left_side = jnp.concatenate(
            [u[pl.ds(at + a * d, R)].reshape(R * WIDE, CH) for a in range(3)], axis=-1
        )
        z = dot(left_side, w[l].reshape(3 * CH, 3 * CH))
        parts = [z[:, b * CH : (b + 1) * CH].reshape(R, WIDE, CH) for b in range(3)]
        return shifted(parts, d)

    def layer0(row):
        new = fx[pl.ds(row + 4, R)].astype(jnp.float32) + conv(u0, row + 3, 1, 0)
        s[pl.ds(row + 2, R)] = new
        u1[pl.ds(row + 2, R)] = norm_act(new, gain(1), mask(row, R))

    def layer1(row):
        new = s[pl.ds(row + 2, R)] + conv(u1, row, 2, 1)
        s[pl.ds(row + 2, R)] = new
        u2[pl.ds(row + 4, R)] = norm_act(new, gain(2), mask(row, R))

    def layer2(row):
        new = s[pl.ds(row + 2, R), :COLS] + conv(u2, row, 4, 2)[:, :COLS]
        s[pl.ds(row + 2, R), :COLS] = new
        act = norm_act(new, gain(3), None)
        u3[pl.ds(row + 8, R)] = act
        at = pl.ds(row8(row), R * 8)
        act = act.astype(jnp.float32)
        pk3[0, at] = flat(act[:, :8])
        pk3[1, at] = flat(act[:, COLS - 8 :])

    weights_here(0)
    loop(3, lambda i: layer0_own(2 + R * i))
    first_received(6)
    first_received(7)
    loop(4, halo_act)
    layer0_halo_dot()
    loop(3, layer0_halo)
    for k in range(6):
        first_received(k)
    loop(2, outer_act)
    unrolled(2, lambda i: layer0(-2 + 16 * i))
    weights_here(1)
    unrolled(2, lambda i: layer1(12 * i))
    second = [
        (u2.at[pl.ds(4, 4)], u2.at[pl.ds(20, 4)], -1, 0),
        (u2.at[pl.ds(16, 4)], u2.at[pl.ds(0, 4)], 1, 0),
    ]
    for k, (src, dst, dr, dc) in enumerate(second):
        send(src, dst, e2_s.at[k], e2_r.at[k], dr, dc)
    unrolled(2, lambda i: layer1(4 + R * i))
    weights_here(2)
    unrolled(2, lambda i: layer2(4 + R * i))
    third = [
        (u3.at[pl.ds(16, 4)], u3.at[pl.ds(0, 4)], 1, 0),
        (u3.at[pl.ds(12, 4)], u3.at[pl.ds(28, 4)], -1, 0),
        (u3.at[pl.ds(20, 4)], u3.at[pl.ds(4, 4)], 1, 0),
        (u3.at[pl.ds(8, 4)], u3.at[pl.ds(24, 4)], -1, 0),
    ]
    third_from = (8, 4, 12, 0)
    third_to = (-8, 20, -4, 16)

    def columns(k):
        for side, dc in ((0, -1), (1, 1)):
            src = pk3.at[side, pl.ds(third_from[k] * 8, 32)]
            here = hb3.at[side, pl.ds((third_from[k] + 8) * 8, 32)]
            corner = hb3.at[side, pl.ds((third_to[k] + 8) * 8, 32)]
            yield src, here, x3_s.at[k, side], x3_r.at[k, side], 0, dc
            yield src, corner, d3_s.at[k, side], d3_r.at[k, side], third[k][2], dc

    def third_send(k):
        src, dst, dr, dc = third[k]
        send(src, dst, e3_s.at[k], e3_r.at[k], dr, dc)
        for args in columns(k):
            send(*args)

    third_send(0)
    third_send(1)
    for k, (src, dst, dr, dc) in enumerate(second):
        received(dst, e2_s.at[k], e2_r.at[k], -dr, -dc)
    unrolled(2, lambda i: layer2(12 * i))
    third_send(2)
    third_send(3)

    def spread_cols(z):
        z = [z[:, b * CH : (b + 1) * CH].reshape(R, COLS, CH) for b in range(3)]
        none = jnp.zeros((R, 8, CH), jnp.float32)
        return (
            jnp.concatenate([none, z[0][:, : COLS - 8]], axis=1)
            + z[1]
            + jnp.concatenate([z[2][:, 8:], none], axis=1)
        )

    def add(row, value):
        s[pl.ds(row + 2, R), :COLS] = s[pl.ds(row + 2, R), :COLS] + value

    def layer3_own(i):
        row = R * i
        low_row = lax.rem(row, 8)
        left_side = jnp.concatenate(
            [u3[pl.ds(8 + low_row + 8 * a, R)].reshape(R * COLS, CH) for a in range(2)], axis=-1
        )
        z = dot(left_side, w[3, pl.ds(1 - row // 8, 2)].reshape(2 * CH, 3 * CH))
        add(row, spread_cols(z))

    def row_of(k):
        even, late = 1 - lax.rem(k, 2), k // 2
        return even * 4 * late + (1 - even) * (12 - 4 * late)

    def move(k, first_axis, action, buf_out, buf_in, ss, rs):
        for parity in range(2):
            dr, dc = (0, 1) if (parity == 0) == first_axis else (HOP, 0)

            @pl.when(lax.rem(k, 2) == parity)
            def _():
                for side, sign in ((0, 1), (1, -1)):
                    if action == "received":
                        received(buf_in.at[k, side], ss.at[k, side], rs.at[k, side], -sign * dr, -sign * dc)
                    else:
                        fn = send if action == "send" else sent
                        src = buf_out.at[k] if first_axis else buf_out.at[k, side]
                        fn(src, buf_in.at[k, side], ss.at[k, side], rs.at[k, side], sign * dr, sign * dc)

    def column_taps(side, rows):
        left_side = jnp.concatenate(
            [
                jnp.concatenate(
                    [hb3[side, pl.ds(pl.multiple_of((row + 8 * a) * 8, 32), R * 8)] for a in range(3)],
                    axis=-1,
                )
                for row in rows
            ],
            axis=0,
        )
        b = 2 if side == 0 else 0
        return dot(left_side, w[3, :, :, b * CH : (b + 1) * CH].reshape(3 * CH, CH))

    def layer3_pair(g):
        rows = (R * g, 12 - R * g)
        from_right = column_taps(0, rows)
        from_left = column_taps(1, rows)
        for odd in range(2):
            k, row = 2 * g + odd, rows[odd]
            z = dot(u3[pl.ds(row + 16 * odd, R)].reshape(R * COLS, CH), w[3, 2 * odd])
            new = s[pl.ds(row + 2, R), :COLS] + spread_cols(z)
            part = slice(odd * R * 8, (odd + 1) * R * 8)
            new = jnp.concatenate(
                [
                    new[:, :8] + from_left[part].reshape(R, 8, CH),
                    new[:, 8 : COLS - 8],
                    new[:, COLS - 8 :] + from_right[part].reshape(R, 8, CH),
                ],
                axis=1,
            )
            s[pl.ds(row + 2, R), :COLS] = new
            fa[k] = norm_act(new, gain(4), None)

    def third_received(k):
        src, dst, dr, dc = third[k]
        received(dst, e3_s.at[k], e3_r.at[k], -dr, -dc)
        for (_, dst, ss, rs, dr, dc) in list(columns(k))[1::2]:
            received(dst, ss, rs, -dr, -dc)

    weights_here(3)
    loop(4, layer3_own)
    weights_here(4)
    weights_here(5)

    for k in range(4):
        for (_, dst, ss, rs, dr, dc) in list(columns(k))[0::2]:
            received(dst, ss, rs, -dr, -dc)

    def far_send(k):
        move(k, True, "send", fa, fr, fa_s, fa_r)

    def far_sent(k):
        move(k, True, "sent", fa, fr, fa_s, fa_r)

    def layer3_turn(g):
        for turn in range(2):
            @pl.when(g == turn)
            def _():
                third_received(2 * turn)
                third_received(2 * turn + 1)

        @pl.when(g == 1)
        def _():
            far_send(0)
            far_send(1)

        layer3_pair(g)

    loop(2, layer3_turn)
    for k in (2, 3):
        far_send(k)

    def far_step(k):
        row = row_of(k)
        move(k, True, "received", fa, fr, fa_s, fa_r)
        left_side = jnp.concatenate(
            [v.reshape(R * COLS, CH) for v in (fr[k, 0], fa[k], fr[k, 1])], axis=-1
        )
        z = dot(left_side, wf[lax.rem(k, 2)].reshape(3 * CH, 3 * CH))
        fp[k, 0] = z[:, :CH].astype(jnp.bfloat16).reshape(R, COLS, CH)
        fp[k, 1] = z[:, 2 * CH :].astype(jnp.bfloat16).reshape(R, COLS, CH)
        move(k, False, "send", fp, fq, fp_s, fp_r)
        add(row, z[:, CH : 2 * CH].reshape(R, COLS, CH))

    loop(4, far_step)

    def far_end(k):
        row = row_of(k)
        move(k, False, "received", fp, fq, fp_s, fp_r)
        far_sum = fq[k, 0].astype(jnp.float32) + fq[k, 1].astype(jnp.float32)
        out[pl.ds(row, R)] = s[pl.ds(row + 2, R), :COLS] + far_sum

    loop(4, far_end)

    for k, (src, dst, dr, dc) in enumerate(first):
        sent(src, dst, e0_s.at[k], e0_r.at[k], dr, dc)
    for k, (src, dst, dr, dc) in enumerate(second):
        sent(src, dst, e2_s.at[k], e2_r.at[k], dr, dc)
    for k, (src, dst, dr, dc) in enumerate(third):
        sent(src, dst, e3_s.at[k], e3_r.at[k], dr, dc)
        for args in columns(k):
            sent(*args)

    def all_sent(k):
        far_sent(k)
        move(k, False, "sent", fp, fq, fp_s, fp_r)

    loop(4, all_sent)


def local(nrow, ncol, features, inner_weights, far_weights, gains):
    bf16, f32 = jnp.bfloat16, jnp.float32
    dma = pltpu.SemaphoreType.DMA
    hbm = pl.BlockSpec(memory_space=pltpu.HBM)
    return pl.pallas_call(
        functools.partial(kernel, nrow, ncol),
        out_shape=jax.ShapeDtypeStruct(features.shape, f32),
        in_specs=[hbm] * 4,
        out_specs=pl.BlockSpec(memory_space=pltpu.VMEM),
        scratch_shapes=[
            pltpu.VMEM(gains.shape, f32),
            pltpu.VMEM((ROWS + 8, WIDE, CH), bf16),
            pltpu.VMEM((2, ROWS * 8, CH), bf16),
            pltpu.VMEM((2, (ROWS + 8) * 8, CH), bf16),
            pltpu.VMEM((ROWS + 8, WIDE, CH), bf16),
            pltpu.VMEM((ROWS + 4, WIDE, CH), bf16),
            pltpu.VMEM((ROWS + 8, WIDE, CH), bf16),
            pltpu.VMEM((ROWS + 16, COLS, CH), bf16),
            pltpu.VMEM((2, ROWS * 8, CH), bf16),
            pltpu.VMEM((2, (ROWS + 16) * 8, CH), bf16),
            pltpu.VMEM((ROWS + 4, WIDE, CH), f32),
            pltpu.VMEM((3 * R, 16, 3 * CH), f32),
            pltpu.VMEM((4, 3, CH, 3 * CH), bf16),
            pltpu.VMEM((2, 3, CH, 3 * CH), bf16),
            pltpu.VMEM((4, R, COLS, CH), bf16),
            pltpu.VMEM((4, 2, R, COLS, CH), bf16),
            pltpu.VMEM((4, 2, R, COLS, CH), bf16),
            pltpu.VMEM((4, 2, R, COLS, CH), bf16),
            dma, dma, dma((6,)),
            dma((8,)), dma((8,)), dma((2,)), dma((2,)), dma((4,)), dma((4,)),
            dma((4, 2)), dma((4, 2)), dma((4, 2)), dma((4, 2)), dma((4, 2)), dma((4, 2)), dma((4, 2)), dma((4, 2)),
        ],
        compiler_params=pltpu.CompilerParams(
            collective_id=0, has_side_effects=True, vmem_limit_bytes=50 * 2**20
        ),
    )(features, inner_weights, far_weights, gains)


def solution(mesh):
    return jax.shard_map(
        functools.partial(local, mesh.shape["row"], mesh.shape["col"]),
        mesh=mesh,
        in_specs=(P("row", "col", None), P(), P(), P()),
        out_specs=P("row", "col", None),
        check_vma=False,
    )
```

```python
import functools

import jax
import jax.numpy as jnp
from jax import lax
from jax.experimental import pallas as pl
from jax.experimental.pallas import tpu as pltpu
from jax.sharding import PartitionSpec as P

MESH = pl.DeviceIdType.MESH
CH = 384
HOP = 4
ROWS, COLS = 16, 64
WIDE = 80
R = 4


def norm_act(stream, gain, mask):
    centre = jnp.mean(stream, axis=-1, keepdims=True)
    moved = stream - centre
    spread = jnp.mean(moved * moved, axis=-1, keepdims=True)
    scale = lax.rsqrt(spread + 1e-05)
    if mask is not None:
        scale = scale * mask
    return jax.nn.gelu(moved * scale * gain).astype(jnp.bfloat16)


def dot(a, b):
    return jnp.dot(a, b, preferred_element_type=jnp.float32)


def row8(row):
    return row * 8 if isinstance(row, int) else pl.multiple_of(row * 8, 32)


def unrolled(n, body):
    for i in range(n):
        body(i)


def loop(n, body):
    def step(i, carry):
        body(i)
        return carry

    lax.fori_loop(0, n, step, 0)


def kernel(
    nrow, ncol,
    feat, inner, far, gains_in, out,
    gains, fx, pk, hb, u0, u1, u2, u3, pk3, hb3, s, zh, w, wf,
    fa, fr, fp, fq,
    in_sem, g_sem, w_sem,
    e0_s, e0_r, e2_s, e2_r, e3_s, e3_r, x3_s, x3_r, d3_s, d3_r, fa_s, fa_r, fp_s, fp_r,
):
    r, c = lax.axis_index("row"), lax.axis_index("col")

    def there(dr, dc):
        return (r + dr >= 0) & (r + dr < nrow) & (c + dc >= 0) & (c + dc < ncol)

    def remote(src, dst, ss, rs, dr, dc):
        return pltpu.make_async_remote_copy(
            src_ref=src, dst_ref=dst, send_sem=ss, recv_sem=rs,
            device_id=(r + dr, c + dc), device_id_type=MESH,
        )

    def send(src, dst, ss, rs, dr, dc):
        @pl.when(there(dr, dc))
        def _():
            remote(src, dst, ss, rs, dr, dc).start()

    def sent(src, dst, ss, rs, dr, dc):
        @pl.when(there(dr, dc))
        def _():
            remote(src, dst, ss, rs, dr, dc).wait_send()

    def received(dst, ss, rs, dr, dc):
        @pl.when(there(dr, dc))
        def _():
            remote(dst, dst, ss, rs, dr, dc).wait_recv()

    own_copy = pltpu.make_async_copy(feat, fx.at[pl.ds(4, ROWS), pl.ds(0, COLS)], in_sem)
    own_copy.start()
    gains_copy = pltpu.make_async_copy(gains_in, gains, g_sem)
    gains_copy.start()

    def weights(l):
        for b in range(3):
            pltpu.make_async_copy(
                inner.at[l, :, b], w.at[l, :, :, pl.ds(b * CH, CH)], w_sem.at[l]
            ).start()

    weights(0)

    greet = [(dr, dc) for dr in (-1, 0, 1) for dc in (-1, 0, 1) if dr or dc] + [(HOP, 0), (-HOP, 0)]
    barrier = pltpu.get_barrier_semaphore()
    for dr, dc in greet:
        @pl.when(there(dr, dc))
        def _():
            pl.semaphore_signal(barrier, inc=1, device_id=(r + dr, c + dc), device_id_type=MESH)


    @pl.when(r == 0)
    def _():
        fx[0:4, :COLS] = jnp.zeros((4, COLS, CH), fx.dtype)
        u2[0:4] = jnp.zeros((4, WIDE, CH), u2.dtype)
        u3[0:8] = jnp.zeros((8, COLS, CH), u3.dtype)
        for side in range(2):
            hb[side, 0:32] = jnp.zeros((32, CH), hb.dtype)
            hb3[side, 0:64] = jnp.zeros((64, CH), hb3.dtype)

    @pl.when(r == nrow - 1)
    def _():
        fx[20:24, :COLS] = jnp.zeros((4, COLS, CH), fx.dtype)
        u2[20:24] = jnp.zeros((4, WIDE, CH), u2.dtype)
        u3[24:32] = jnp.zeros((8, COLS, CH), u3.dtype)
        for side in range(2):
            hb[side, 160:192] = jnp.zeros((32, CH), hb.dtype)
            hb3[side, 192:256] = jnp.zeros((64, CH), hb3.dtype)

    tile_zero = jnp.zeros((R, COLS, CH), jnp.bfloat16)

    @pl.when(c == 0)
    def _():
        hb[1] = jnp.zeros((192, CH), hb.dtype)
        hb3[1] = jnp.zeros((256, CH), hb3.dtype)
        for k in range(4):
            (fr if k % 2 == 0 else fq)[k, 0] = tile_zero

    @pl.when(c == ncol - 1)
    def _():
        hb[0] = jnp.zeros((192, CH), hb.dtype)
        hb3[0] = jnp.zeros((256, CH), hb3.dtype)
        for k in range(4):
            (fr if k % 2 == 0 else fq)[k, 1] = tile_zero

    @pl.when(r < HOP)
    def _():
        for k in range(4):
            (fr if k % 2 == 1 else fq)[k, 0] = tile_zero

    @pl.when(r >= nrow - HOP)
    def _():
        for k in range(4):
            (fr if k % 2 == 1 else fq)[k, 1] = tile_zero

    def gain(l):
        return gains[l : l + 1, :][None]

    def flat(value):
        n = value.shape[0]
        return value.reshape(n * 8, CH).astype(jnp.bfloat16)

    def unflat(ref, side, row, n):
        at = pl.multiple_of(row * 8, 16)
        return ref[side, pl.ds(at, n * 8)].astype(jnp.float32).reshape(n, 8, CH)

    def own_act(i):
        row = R * i
        value = fx[pl.ds(row + 4, R), :COLS].astype(jnp.float32)
        at = pl.ds(row8(row), R * 8)
        pk[0, at] = flat(value[:, :8])
        pk[1, at] = flat(value[:, COLS - 8 :])
        u0[pl.ds(row + 4, R), :COLS] = norm_act(value, gain(0), None)

    gains_copy.wait()
    own_copy.wait()
    loop(4, own_act)
    pl.semaphore_wait(barrier, sum(jnp.where(there(dr, dc), 1, 0) for dr, dc in greet))

    own = pl.ds(0, COLS)
    top, mid, bottom = pl.ds(0, 32), pl.ds(32, ROWS * 8), pl.ds(160, 32)
    head, tail = pl.ds(0, 32), pl.ds(96, 32)
    first = [
        (feat.at[pl.ds(0, 3)], fx.at[pl.ds(20, 3), own], -1, 0),
        (feat.at[pl.ds(13, 3)], fx.at[pl.ds(1, 3), own], 1, 0),
        (pk.at[0, head], hb.at[0, bottom], -1, -1),
        (pk.at[1, head], hb.at[1, bottom], -1, 1),
        (pk.at[0, tail], hb.at[0, top], 1, -1),
        (pk.at[1, tail], hb.at[1, top], 1, 1),
        (pk.at[0], hb.at[0, mid], 0, -1),
        (pk.at[1], hb.at[1, mid], 0, 1),
    ]
    for k, (src, dst, dr, dc) in enumerate(first):
        send(src, dst, e0_s.at[k], e0_r.at[k], dr, dc)

    def first_received(k):
        _, dst, dr, dc = first[k]
        received(dst, e0_s.at[k], e0_r.at[k], -dr, -dc)

    for l in range(1, 4):
        weights(l)
    for t in range(3):
        place = pl.ds((0, 2, 1)[t] * CH, CH)
        pltpu.make_async_copy(far.at[t], wf.at[0, :, :, place], w_sem.at[4]).start()
        pltpu.make_async_copy(far.at[:, t], wf.at[1, :, :, place], w_sem.at[5]).start()

    def weights_here(l):
        ref = w.at[l] if l < 4 else wf.at[l - 4]
        pltpu.make_async_copy(ref, ref, w_sem.at[l]).wait()

    def mask(row, n):
        rows = row + lax.broadcasted_iota(jnp.int32, (n, WIDE, 1), 0)
        cols = lax.broadcasted_iota(jnp.int32, (n, WIDE, 1), 1)
        row_from = jnp.where(r == 0, 0, -8)
        row_to = jnp.where(r == nrow - 1, ROWS, ROWS + 8)
        col_from = jnp.where(c == ncol - 1, COLS + 8, COLS)
        col_to = jnp.where(c == 0, COLS + 8, WIDE)
        inside = (rows >= row_from) & (rows < row_to)
        inside = inside & ((cols < COLS) | ((cols >= col_from) & (cols < col_to)))
        return jnp.where(inside, 1.0, 0.0).astype(jnp.float32)

    def halo_cols(row, n):
        return jnp.concatenate([unflat(hb, 0, row + 4, n), unflat(hb, 1, row + 4, n)], axis=1)

    def halo_act(i):
        row = R * i
        halo = halo_cols(row, R)
        fx[pl.ds(row + 4, R), COLS:] = halo.astype(jnp.bfloat16)
        u0[pl.ds(row + 4, R), COLS:] = norm_act(halo, gain(0), None)

    def outer_act(i):
        row = 20 * i - 4
        halo = halo_cols(row, R)
        fx[pl.ds(row + 4, R), COLS:] = halo.astype(jnp.bfloat16)
        value = jnp.concatenate([fx[pl.ds(row + 4, R), :COLS].astype(jnp.float32), halo], axis=1)
        u0[pl.ds(row + 4, R)] = norm_act(value, gain(0), None)

    def shifted(parts, d):
        return pltpu.roll(parts[0], d, 1) + parts[1] + pltpu.roll(parts[2], WIDE - d, 1)

    def layer0_own(row):
        left_side = jnp.concatenate(
            [u0[pl.ds(row + 3 + a, R), :COLS].reshape(R * COLS, CH) for a in range(3)], axis=-1
        )
        z = dot(left_side, w[0].reshape(3 * CH, 3 * CH))
        none = jnp.zeros((R, WIDE - COLS, CH), jnp.float32)
        parts = [
            jnp.concatenate([z[:, b * CH : (b + 1) * CH].reshape(R, COLS, CH), none], axis=1)
            for b in range(3)
        ]
        s[pl.ds(row + 2, R)] = shifted(parts, 1)

    def layer0_halo_dot():
        n = 3 * R
        left_side = jnp.concatenate(
            [u0[pl.ds(5 + a, n), COLS:].reshape(n * 16, CH) for a in range(3)], axis=-1
        )
        zh[...] = dot(left_side, w[0].reshape(3 * CH, 3 * CH)).reshape(n, 16, 3 * CH)

    def layer0_halo(i):
        row = 2 + R * i
        z = zh[pl.ds(R * i, R)]
        none = jnp.zeros((R, COLS, CH), jnp.float32)
        parts = [jnp.concatenate([none, z[:, :, b * CH : (b + 1) * CH]], axis=1) for b in range(3)]
        new = fx[pl.ds(row + 4, R)].astype(jnp.float32) + s[pl.ds(row + 2, R)] + shifted(parts, 1)
        s[pl.ds(row + 2, R)] = new
        u1[pl.ds(row + 2, R)] = norm_act(new, gain(1), mask(row, R))

    def conv(u, at, d, l):
        left_side = jnp.concatenate(
            [u[pl.ds(at + a * d, R)].reshape(R * WIDE, CH) for a in range(3)], axis=-1
        )
        z = dot(left_side, w[l].reshape(3 * CH, 3 * CH))
        parts = [z[:, b * CH : (b + 1) * CH].reshape(R, WIDE, CH) for b in range(3)]
        return shifted(parts, d)

    def layer0(row):
        new = fx[pl.ds(row + 4, R)].astype(jnp.float32) + conv(u0, row + 3, 1, 0)
        s[pl.ds(row + 2, R)] = new
        u1[pl.ds(row + 2, R)] = norm_act(new, gain(1), mask(row, R))

    def layer1(row):
        new = s[pl.ds(row + 2, R)] + conv(u1, row, 2, 1)
        s[pl.ds(row + 2, R)] = new
        u2[pl.ds(row + 4, R)] = norm_act(new, gain(2), mask(row, R))

    def layer2(row):
        new = s[pl.ds(row + 2, R), :COLS] + conv(u2, row, 4, 2)[:, :COLS]
        s[pl.ds(row + 2, R), :COLS] = new
        act = norm_act(new, gain(3), None)
        u3[pl.ds(row + 8, R)] = act
        at = pl.ds(row8(row), R * 8)
        act = act.astype(jnp.float32)
        pk3[0, at] = flat(act[:, :8])
        pk3[1, at] = flat(act[:, COLS - 8 :])

    weights_here(0)
    loop(3, lambda i: layer0_own(2 + R * i))
    first_received(6)
    first_received(7)
    loop(4, halo_act)
    layer0_halo_dot()
    loop(3, layer0_halo)
    for k in range(6):
        first_received(k)
    loop(2, outer_act)
    unrolled(2, lambda i: layer0(-2 + 16 * i))
    weights_here(1)
    unrolled(2, lambda i: layer1(12 * i))
    second = [
        (u2.at[pl.ds(4, 4)], u2.at[pl.ds(20, 4)], -1, 0),
        (u2.at[pl.ds(16, 4)], u2.at[pl.ds(0, 4)], 1, 0),
    ]
    for k, (src, dst, dr, dc) in enumerate(second):
        send(src, dst, e2_s.at[k], e2_r.at[k], dr, dc)
    unrolled(2, lambda i: layer1(4 + R * i))
    weights_here(2)
    unrolled(2, lambda i: layer2(4 + R * i))
    third = [
        (u3.at[pl.ds(16, 4)], u3.at[pl.ds(0, 4)], 1, 0),
        (u3.at[pl.ds(12, 4)], u3.at[pl.ds(28, 4)], -1, 0),
        (u3.at[pl.ds(20, 4)], u3.at[pl.ds(4, 4)], 1, 0),
        (u3.at[pl.ds(8, 4)], u3.at[pl.ds(24, 4)], -1, 0),
    ]
    third_from = (8, 4, 12, 0)
    third_to = (-8, 20, -4, 16)

    def columns(k):
        for side, dc in ((0, -1), (1, 1)):
            src = pk3.at[side, pl.ds(third_from[k] * 8, 32)]
            here = hb3.at[side, pl.ds((third_from[k] + 8) * 8, 32)]
            corner = hb3.at[side, pl.ds((third_to[k] + 8) * 8, 32)]
            yield src, here, x3_s.at[k, side], x3_r.at[k, side], 0, dc
            yield src, corner, d3_s.at[k, side], d3_r.at[k, side], third[k][2], dc

    def third_send(*steps):
        for k in steps:
            src, dst, dr, dc = third[k]
            send(src, dst, e3_s.at[k], e3_r.at[k], dr, dc)
        for k in steps:
            for args in columns(k):
                send(*args)

    third_send(0, 1)
    for k, (src, dst, dr, dc) in enumerate(second):
        received(dst, e2_s.at[k], e2_r.at[k], -dr, -dc)
    unrolled(2, lambda i: layer2(12 * i))
    third_send(2, 3)

    def spread_cols(z):
        z = [z[:, b * CH : (b + 1) * CH].reshape(R, COLS, CH) for b in range(3)]
        none = jnp.zeros((R, 8, CH), jnp.float32)
        return (
            jnp.concatenate([none, z[0][:, : COLS - 8]], axis=1)
            + z[1]
            + jnp.concatenate([z[2][:, 8:], none], axis=1)
        )

    def add(row, value):
        s[pl.ds(row + 2, R), :COLS] = s[pl.ds(row + 2, R), :COLS] + value

    def layer3_own(i):
        row = R * i
        low_row = lax.rem(row, 8)
        left_side = jnp.concatenate(
            [u3[pl.ds(8 + low_row + 8 * a, R)].reshape(R * COLS, CH) for a in range(2)], axis=-1
        )
        z = dot(left_side, w[3, pl.ds(1 - row // 8, 2)].reshape(2 * CH, 3 * CH))
        add(row, spread_cols(z))

    def row_of(k):
        even, late = 1 - lax.rem(k, 2), k // 2
        return even * 4 * late + (1 - even) * (12 - 4 * late)

    def move(k, first_axis, action, buf_out, buf_in, ss, rs):
        for parity in range(2):
            dr, dc = (0, 1) if (parity == 0) == first_axis else (HOP, 0)

            @pl.when(lax.rem(k, 2) == parity)
            def _():
                for side, sign in ((0, 1), (1, -1)):
                    if action == "received":
                        received(buf_in.at[k, side], ss.at[k, side], rs.at[k, side], -sign * dr, -sign * dc)
                    else:
                        fn = send if action == "send" else sent
                        src = buf_out.at[k] if first_axis else buf_out.at[k, side]
                        fn(src, buf_in.at[k, side], ss.at[k, side], rs.at[k, side], sign * dr, sign * dc)

    def column_taps(side, rows):
        left_side = jnp.concatenate(
            [
                jnp.concatenate(
                    [hb3[side, pl.ds(pl.multiple_of((row + 8 * a) * 8, 32), R * 8)] for a in range(3)],
                    axis=-1,
                )
                for row in rows
            ],
            axis=0,
        )
        b = 2 if side == 0 else 0
        return dot(left_side, w[3, :, :, b * CH : (b + 1) * CH].reshape(3 * CH, CH))

    def layer3_pair(g):
        rows = (R * g, 12 - R * g)
        from_right = column_taps(0, rows)
        from_left = column_taps(1, rows)
        for odd in range(2):
            k, row = 2 * g + odd, rows[odd]
            z = dot(u3[pl.ds(row + 16 * odd, R)].reshape(R * COLS, CH), w[3, 2 * odd])
            new = s[pl.ds(row + 2, R), :COLS] + spread_cols(z)
            part = slice(odd * R * 8, (odd + 1) * R * 8)
            new = jnp.concatenate(
                [
                    new[:, :8] + from_left[part].reshape(R, 8, CH),
                    new[:, 8 : COLS - 8],
                    new[:, COLS - 8 :] + from_right[part].reshape(R, 8, CH),
                ],
                axis=1,
            )
            s[pl.ds(row + 2, R), :COLS] = new
            fa[k] = norm_act(new, gain(4), None)

    def third_received(k):
        src, dst, dr, dc = third[k]
        received(dst, e3_s.at[k], e3_r.at[k], -dr, -dc)
        for (_, dst, ss, rs, dr, dc) in list(columns(k))[1::2]:
            received(dst, ss, rs, -dr, -dc)

    weights_here(3)
    loop(4, layer3_own)
    weights_here(4)
    weights_here(5)

    for k in range(4):
        for (_, dst, ss, rs, dr, dc) in list(columns(k))[0::2]:
            received(dst, ss, rs, -dr, -dc)

    def far_send(k):
        move(k, True, "send", fa, fr, fa_s, fa_r)

    def far_sent(k):
        move(k, True, "sent", fa, fr, fa_s, fa_r)

    def layer3_turn(g):
        for turn in range(2):
            @pl.when(g == turn)
            def _():
                third_received(2 * turn)
                third_received(2 * turn + 1)

        @pl.when(g == 1)
        def _():
            far_send(0)
            far_send(1)

        layer3_pair(g)

    loop(2, layer3_turn)
    for k in (2, 3):
        far_send(k)

    def far_step(k):
        row = row_of(k)
        move(k, True, "received", fa, fr, fa_s, fa_r)
        left_side = jnp.concatenate(
            [v.reshape(R * COLS, CH) for v in (fr[k, 0], fa[k], fr[k, 1])], axis=-1
        )
        weight = wf[lax.rem(k, 2)].reshape(3 * CH, 3 * CH)
        z = dot(left_side, weight[:, : 2 * CH])
        fp[k, 0] = z[:, :CH].astype(jnp.bfloat16).reshape(R, COLS, CH)
        fp[k, 1] = z[:, CH :].astype(jnp.bfloat16).reshape(R, COLS, CH)
        move(k, False, "send", fp, fq, fp_s, fp_r)
        add(row, dot(left_side, weight[:, 2 * CH :]).reshape(R, COLS, CH))

    loop(4, far_step)

    def far_end(k):
        row = row_of(k)
        move(k, False, "received", fp, fq, fp_s, fp_r)
        far_sum = fq[k, 0].astype(jnp.float32) + fq[k, 1].astype(jnp.float32)
        out[pl.ds(row, R)] = s[pl.ds(row + 2, R), :COLS] + far_sum

    loop(4, far_end)

    for k, (src, dst, dr, dc) in enumerate(first):
        sent(src, dst, e0_s.at[k], e0_r.at[k], dr, dc)
    for k, (src, dst, dr, dc) in enumerate(second):
        sent(src, dst, e2_s.at[k], e2_r.at[k], dr, dc)
    for k, (src, dst, dr, dc) in enumerate(third):
        sent(src, dst, e3_s.at[k], e3_r.at[k], dr, dc)
        for args in columns(k):
            sent(*args)

    def all_sent(k):
        far_sent(k)
        move(k, False, "sent", fp, fq, fp_s, fp_r)

    loop(4, all_sent)


def local(nrow, ncol, features, inner_weights, far_weights, gains):
    bf16, f32 = jnp.bfloat16, jnp.float32
    dma = pltpu.SemaphoreType.DMA
    hbm = pl.BlockSpec(memory_space=pltpu.HBM)
    return pl.pallas_call(
        functools.partial(kernel, nrow, ncol),
        out_shape=jax.ShapeDtypeStruct(features.shape, f32),
        in_specs=[hbm] * 4,
        out_specs=pl.BlockSpec(memory_space=pltpu.VMEM),
        scratch_shapes=[
            pltpu.VMEM(gains.shape, f32),
            pltpu.VMEM((ROWS + 8, WIDE, CH), bf16),
            pltpu.VMEM((2, ROWS * 8, CH), bf16),
            pltpu.VMEM((2, (ROWS + 8) * 8, CH), bf16),
            pltpu.VMEM((ROWS + 8, WIDE, CH), bf16),
            pltpu.VMEM((ROWS + 4, WIDE, CH), bf16),
            pltpu.VMEM((ROWS + 8, WIDE, CH), bf16),
            pltpu.VMEM((ROWS + 16, COLS, CH), bf16),
            pltpu.VMEM((2, ROWS * 8, CH), bf16),
            pltpu.VMEM((2, (ROWS + 16) * 8, CH), bf16),
            pltpu.VMEM((ROWS + 4, WIDE, CH), f32),
            pltpu.VMEM((3 * R, 16, 3 * CH), f32),
            pltpu.VMEM((4, 3, CH, 3 * CH), bf16),
            pltpu.VMEM((2, 3, CH, 3 * CH), bf16),
            pltpu.VMEM((4, R, COLS, CH), bf16),
            pltpu.VMEM((4, 2, R, COLS, CH), bf16),
            pltpu.VMEM((4, 2, R, COLS, CH), bf16),
            pltpu.VMEM((4, 2, R, COLS, CH), bf16),
            dma, dma, dma((6,)),
            dma((8,)), dma((8,)), dma((2,)), dma((2,)), dma((4,)), dma((4,)),
            dma((4, 2)), dma((4, 2)), dma((4, 2)), dma((4, 2)), dma((4, 2)), dma((4, 2)), dma((4, 2)), dma((4, 2)),
        ],
        compiler_params=pltpu.CompilerParams(
            collective_id=0, has_side_effects=True, vmem_limit_bytes=50 * 2**20
        ),
    )(features, inner_weights, far_weights, gains)


def solution(mesh):
    return jax.shard_map(
        functools.partial(local, mesh.shape["row"], mesh.shape["col"]),
        mesh=mesh,
        in_specs=(P("row", "col", None), P(), P(), P()),
        out_specs=P("row", "col", None),
        check_vma=False,
    )
```

```python
import functools

import jax
import jax.numpy as jnp
from jax import lax
from jax.experimental import pallas as pl
from jax.experimental.pallas import tpu as pltpu
from jax.sharding import PartitionSpec as P

MESH = pl.DeviceIdType.MESH
CH = 384
HOP = 4
ROWS, COLS = 16, 64
WIDE = 80
R = 4


def norm_act(stream, gain, mask):
    centre = jnp.mean(stream, axis=-1, keepdims=True)
    moved = stream - centre
    spread = jnp.mean(moved * moved, axis=-1, keepdims=True)
    scale = lax.rsqrt(spread + 1e-05)
    if mask is not None:
        scale = scale * mask
    return jax.nn.gelu(moved * scale * gain).astype(jnp.bfloat16)


def dot(a, b):
    return jnp.dot(a, b, preferred_element_type=jnp.float32)


def row8(row):
    return row * 8 if isinstance(row, int) else pl.multiple_of(row * 8, 32)


def unrolled(n, body):
    for i in range(n):
        body(i)


def loop(n, body):
    def step(i, carry):
        body(i)
        return carry

    lax.fori_loop(0, n, step, 0)


def kernel(
    nrow, ncol,
    feat, inner, far, gains_in, out,
    gains, fx, pk, hb, u0, u1, u2, u3, pk3, hb3, s, zh, w, wf,
    fa, fr, fp, fq,
    in_sem, g_sem, w_sem,
    e0_s, e0_r, e2_s, e2_r, e3_s, e3_r, x3_s, x3_r, d3_s, d3_r, fa_s, fa_r, fp_s, fp_r,
):
    r, c = lax.axis_index("row"), lax.axis_index("col")

    def there(dr, dc):
        return (r + dr >= 0) & (r + dr < nrow) & (c + dc >= 0) & (c + dc < ncol)

    def remote(src, dst, ss, rs, dr, dc):
        return pltpu.make_async_remote_copy(
            src_ref=src, dst_ref=dst, send_sem=ss, recv_sem=rs,
            device_id=(r + dr, c + dc), device_id_type=MESH,
        )

    def send(src, dst, ss, rs, dr, dc):
        @pl.when(there(dr, dc))
        def _():
            remote(src, dst, ss, rs, dr, dc).start()

    def sent(src, dst, ss, rs, dr, dc):
        @pl.when(there(dr, dc))
        def _():
            remote(src, dst, ss, rs, dr, dc).wait_send()

    def received(dst, ss, rs, dr, dc):
        @pl.when(there(dr, dc))
        def _():
            remote(dst, dst, ss, rs, dr, dc).wait_recv()

    own_copy = pltpu.make_async_copy(feat, fx.at[pl.ds(4, ROWS), pl.ds(0, COLS)], in_sem)
    own_copy.start()
    gains_copy = pltpu.make_async_copy(gains_in, gains, g_sem)
    gains_copy.start()

    def weights(l):
        for b in range(3):
            pltpu.make_async_copy(
                inner.at[l, :, b], w.at[l, :, :, pl.ds(b * CH, CH)], w_sem.at[l]
            ).start()

    weights(0)

    greet = [(dr, dc) for dr in (-1, 0, 1) for dc in (-1, 0, 1) if dr or dc] + [(HOP, 0), (-HOP, 0)]
    barrier = pltpu.get_barrier_semaphore()
    for dr, dc in greet:
        @pl.when(there(dr, dc))
        def _():
            pl.semaphore_signal(barrier, inc=1, device_id=(r + dr, c + dc), device_id_type=MESH)


    @pl.when(r == 0)
    def _():
        fx[0:4, :COLS] = jnp.zeros((4, COLS, CH), fx.dtype)
        u2[0:4] = jnp.zeros((4, WIDE, CH), u2.dtype)
        u3[0:8] = jnp.zeros((8, COLS, CH), u3.dtype)
        for side in range(2):
            hb[side, 0:32] = jnp.zeros((32, CH), hb.dtype)
            hb3[side, 0:64] = jnp.zeros((64, CH), hb3.dtype)

    @pl.when(r == nrow - 1)
    def _():
        fx[20:24, :COLS] = jnp.zeros((4, COLS, CH), fx.dtype)
        u2[20:24] = jnp.zeros((4, WIDE, CH), u2.dtype)
        u3[24:32] = jnp.zeros((8, COLS, CH), u3.dtype)
        for side in range(2):
            hb[side, 160:192] = jnp.zeros((32, CH), hb.dtype)
            hb3[side, 192:256] = jnp.zeros((64, CH), hb3.dtype)

    tile_zero = jnp.zeros((R, COLS, CH), jnp.bfloat16)

    @pl.when(c == 0)
    def _():
        hb[1] = jnp.zeros((192, CH), hb.dtype)
        hb3[1] = jnp.zeros((256, CH), hb3.dtype)
        for k in range(4):
            (fr if k % 2 == 0 else fq)[k, 0] = tile_zero

    @pl.when(c == ncol - 1)
    def _():
        hb[0] = jnp.zeros((192, CH), hb.dtype)
        hb3[0] = jnp.zeros((256, CH), hb3.dtype)
        for k in range(4):
            (fr if k % 2 == 0 else fq)[k, 1] = tile_zero

    @pl.when(r < HOP)
    def _():
        for k in range(4):
            (fr if k % 2 == 1 else fq)[k, 0] = tile_zero

    @pl.when(r >= nrow - HOP)
    def _():
        for k in range(4):
            (fr if k % 2 == 1 else fq)[k, 1] = tile_zero

    def gain(l):
        return gains[l : l + 1, :][None]

    def flat(value):
        n = value.shape[0]
        return value.reshape(n * 8, CH).astype(jnp.bfloat16)

    def unflat(ref, side, row, n):
        at = pl.multiple_of(row * 8, 16)
        return ref[side, pl.ds(at, n * 8)].astype(jnp.float32).reshape(n, 8, CH)

    def own_act(i):
        row = R * i
        value = fx[pl.ds(row + 4, R), :COLS].astype(jnp.float32)
        at = pl.ds(row8(row), R * 8)
        pk[0, at] = flat(value[:, :8])
        pk[1, at] = flat(value[:, COLS - 8 :])
        u0[pl.ds(row + 4, R), :COLS] = norm_act(value, gain(0), None)

    gains_copy.wait()
    own_copy.wait()
    loop(4, own_act)
    pl.semaphore_wait(barrier, sum(jnp.where(there(dr, dc), 1, 0) for dr, dc in greet))

    own = pl.ds(0, COLS)
    top, mid, bottom = pl.ds(0, 32), pl.ds(32, ROWS * 8), pl.ds(160, 32)
    head, tail = pl.ds(0, 32), pl.ds(96, 32)
    first = [
        (feat.at[pl.ds(0, 3)], fx.at[pl.ds(20, 3), own], -1, 0),
        (feat.at[pl.ds(13, 3)], fx.at[pl.ds(1, 3), own], 1, 0),
        (pk.at[0, head], hb.at[0, bottom], -1, -1),
        (pk.at[1, head], hb.at[1, bottom], -1, 1),
        (pk.at[0, tail], hb.at[0, top], 1, -1),
        (pk.at[1, tail], hb.at[1, top], 1, 1),
        (pk.at[0], hb.at[0, mid], 0, -1),
        (pk.at[1], hb.at[1, mid], 0, 1),
    ]
    for k, (src, dst, dr, dc) in enumerate(first):
        send(src, dst, e0_s.at[k], e0_r.at[k], dr, dc)

    def first_received(k):
        _, dst, dr, dc = first[k]
        received(dst, e0_s.at[k], e0_r.at[k], -dr, -dc)

    for l in range(1, 4):
        weights(l)
    for t in range(3):
        place = pl.ds((0, 2, 1)[t] * CH, CH)
        pltpu.make_async_copy(far.at[t], wf.at[0, :, :, place], w_sem.at[4]).start()
        pltpu.make_async_copy(far.at[:, t], wf.at[1, :, :, place], w_sem.at[5]).start()

    def weights_here(l):
        ref = w.at[l] if l < 4 else wf.at[l - 4]
        pltpu.make_async_copy(ref, ref, w_sem.at[l]).wait()

    def mask(row, n):
        rows = row + lax.broadcasted_iota(jnp.int32, (n, WIDE, 1), 0)
        cols = lax.broadcasted_iota(jnp.int32, (n, WIDE, 1), 1)
        row_from = jnp.where(r == 0, 0, -8)
        row_to = jnp.where(r == nrow - 1, ROWS, ROWS + 8)
        col_from = jnp.where(c == ncol - 1, COLS + 8, COLS)
        col_to = jnp.where(c == 0, COLS + 8, WIDE)
        inside = (rows >= row_from) & (rows < row_to)
        inside = inside & ((cols < COLS) | ((cols >= col_from) & (cols < col_to)))
        return jnp.where(inside, 1.0, 0.0).astype(jnp.float32)

    def halo_cols(row, n):
        return jnp.concatenate([unflat(hb, 0, row + 4, n), unflat(hb, 1, row + 4, n)], axis=1)

    def halo_act(i):
        row = R * i
        halo = halo_cols(row, R)
        fx[pl.ds(row + 4, R), COLS:] = halo.astype(jnp.bfloat16)
        u0[pl.ds(row + 4, R), COLS:] = norm_act(halo, gain(0), None)

    def outer_act(i):
        row = 20 * i - 4
        halo = halo_cols(row, R)
        fx[pl.ds(row + 4, R), COLS:] = halo.astype(jnp.bfloat16)
        value = jnp.concatenate([fx[pl.ds(row + 4, R), :COLS].astype(jnp.float32), halo], axis=1)
        u0[pl.ds(row + 4, R)] = norm_act(value, gain(0), None)

    def shifted(parts, d):
        return pltpu.roll(parts[0], d, 1) + parts[1] + pltpu.roll(parts[2], WIDE - d, 1)

    def layer0_own(row):
        left_side = jnp.concatenate(
            [u0[pl.ds(row + 3 + a, R), :COLS].reshape(R * COLS, CH) for a in range(3)], axis=-1
        )
        z = dot(left_side, w[0].reshape(3 * CH, 3 * CH))
        none = jnp.zeros((R, WIDE - COLS, CH), jnp.float32)
        parts = [
            jnp.concatenate([z[:, b * CH : (b + 1) * CH].reshape(R, COLS, CH), none], axis=1)
            for b in range(3)
        ]
        s[pl.ds(row + 2, R)] = shifted(parts, 1)

    def layer0_halo_dot():
        n = 3 * R
        left_side = jnp.concatenate(
            [u0[pl.ds(5 + a, n), COLS:].reshape(n * 16, CH) for a in range(3)], axis=-1
        )
        zh[...] = dot(left_side, w[0].reshape(3 * CH, 3 * CH)).reshape(n, 16, 3 * CH)

    def layer0_halo(i):
        row = 2 + R * i
        z = zh[pl.ds(R * i, R)]
        none = jnp.zeros((R, COLS, CH), jnp.float32)
        parts = [jnp.concatenate([none, z[:, :, b * CH : (b + 1) * CH]], axis=1) for b in range(3)]
        new = fx[pl.ds(row + 4, R)].astype(jnp.float32) + s[pl.ds(row + 2, R)] + shifted(parts, 1)
        s[pl.ds(row + 2, R)] = new
        u1[pl.ds(row + 2, R)] = norm_act(new, gain(1), mask(row, R))

    def conv(u, at, d, l):
        left_side = jnp.concatenate(
            [u[pl.ds(at + a * d, R)].reshape(R * WIDE, CH) for a in range(3)], axis=-1
        )
        z = dot(left_side, w[l].reshape(3 * CH, 3 * CH))
        parts = [z[:, b * CH : (b + 1) * CH].reshape(R, WIDE, CH) for b in range(3)]
        return shifted(parts, d)

    def layer0(row):
        new = fx[pl.ds(row + 4, R)].astype(jnp.float32) + conv(u0, row + 3, 1, 0)
        s[pl.ds(row + 2, R)] = new
        u1[pl.ds(row + 2, R)] = norm_act(new, gain(1), mask(row, R))

    def layer1(row):
        new = s[pl.ds(row + 2, R)] + conv(u1, row, 2, 1)
        s[pl.ds(row + 2, R)] = new
        u2[pl.ds(row + 4, R)] = norm_act(new, gain(2), mask(row, R))

    def layer2(row):
        new = s[pl.ds(row + 2, R), :COLS] + conv(u2, row, 4, 2)[:, :COLS]
        s[pl.ds(row + 2, R), :COLS] = new
        act = norm_act(new, gain(3), None)
        u3[pl.ds(row + 8, R)] = act
        at = pl.ds(row8(row), R * 8)
        act = act.astype(jnp.float32)
        pk3[0, at] = flat(act[:, :8])
        pk3[1, at] = flat(act[:, COLS - 8 :])

    weights_here(0)
    unrolled(3, lambda i: layer0_own(2 + R * i))
    first_received(6)
    first_received(7)
    loop(4, halo_act)
    layer0_halo_dot()
    unrolled(3, layer0_halo)
    for k in range(6):
        first_received(k)
    loop(2, outer_act)
    unrolled(2, lambda i: layer0(-2 + 16 * i))
    weights_here(1)
    unrolled(2, lambda i: layer1(12 * i))
    second = [
        (u2.at[pl.ds(4, 4)], u2.at[pl.ds(20, 4)], -1, 0),
        (u2.at[pl.ds(16, 4)], u2.at[pl.ds(0, 4)], 1, 0),
    ]
    for k, (src, dst, dr, dc) in enumerate(second):
        send(src, dst, e2_s.at[k], e2_r.at[k], dr, dc)
    unrolled(2, lambda i: layer1(4 + R * i))
    weights_here(2)
    unrolled(2, lambda i: layer2(4 + R * i))
    third = [
        (u3.at[pl.ds(16, 4)], u3.at[pl.ds(0, 4)], 1, 0),
        (u3.at[pl.ds(12, 4)], u3.at[pl.ds(28, 4)], -1, 0),
        (u3.at[pl.ds(20, 4)], u3.at[pl.ds(4, 4)], 1, 0),
        (u3.at[pl.ds(8, 4)], u3.at[pl.ds(24, 4)], -1, 0),
    ]
    third_from = (8, 4, 12, 0)
    third_to = (-8, 20, -4, 16)

    def columns(k):
        for side, dc in ((0, -1), (1, 1)):
            src = pk3.at[side, pl.ds(third_from[k] * 8, 32)]
            here = hb3.at[side, pl.ds((third_from[k] + 8) * 8, 32)]
            corner = hb3.at[side, pl.ds((third_to[k] + 8) * 8, 32)]
            yield src, here, x3_s.at[k, side], x3_r.at[k, side], 0, dc
            yield src, corner, d3_s.at[k, side], d3_r.at[k, side], third[k][2], dc

    def third_send(*steps):
        for k in steps:
            src, dst, dr, dc = third[k]
            send(src, dst, e3_s.at[k], e3_r.at[k], dr, dc)
        for k in steps:
            for args in columns(k):
                send(*args)

    third_send(0, 1)
    for k, (src, dst, dr, dc) in enumerate(second):
        received(dst, e2_s.at[k], e2_r.at[k], -dr, -dc)
    unrolled(2, lambda i: layer2(12 * i))
    third_send(2, 3)

    def spread_cols(z):
        z = [z[:, b * CH : (b + 1) * CH].reshape(R, COLS, CH) for b in range(3)]
        none = jnp.zeros((R, 8, CH), jnp.float32)
        return (
            jnp.concatenate([none, z[0][:, : COLS - 8]], axis=1)
            + z[1]
            + jnp.concatenate([z[2][:, 8:], none], axis=1)
        )

    def add(row, value):
        s[pl.ds(row + 2, R), :COLS] = s[pl.ds(row + 2, R), :COLS] + value

    def layer3_own(i):
        row = R * i
        low_row = lax.rem(row, 8)
        left_side = jnp.concatenate(
            [u3[pl.ds(8 + low_row + 8 * a, R)].reshape(R * COLS, CH) for a in range(2)], axis=-1
        )
        z = dot(left_side, w[3, pl.ds(1 - row // 8, 2)].reshape(2 * CH, 3 * CH))
        add(row, spread_cols(z))

    def row_of(k):
        even, late = 1 - lax.rem(k, 2), k // 2
        return even * 4 * late + (1 - even) * (12 - 4 * late)

    def move(k, first_axis, action, buf_out, buf_in, ss, rs):
        for parity in range(2):
            dr, dc = (0, 1) if (parity == 0) == first_axis else (HOP, 0)

            @pl.when(lax.rem(k, 2) == parity)
            def _():
                for side, sign in ((0, 1), (1, -1)):
                    if action == "received":
                        received(buf_in.at[k, side], ss.at[k, side], rs.at[k, side], -sign * dr, -sign * dc)
                    else:
                        fn = send if action == "send" else sent
                        src = buf_out.at[k] if first_axis else buf_out.at[k, side]
                        fn(src, buf_in.at[k, side], ss.at[k, side], rs.at[k, side], sign * dr, sign * dc)

    def column_taps(side, rows):
        left_side = jnp.concatenate(
            [
                jnp.concatenate(
                    [hb3[side, pl.ds(pl.multiple_of((row + 8 * a) * 8, 32), R * 8)] for a in range(3)],
                    axis=-1,
                )
                for row in rows
            ],
            axis=0,
        )
        b = 2 if side == 0 else 0
        return dot(left_side, w[3, :, :, b * CH : (b + 1) * CH].reshape(3 * CH, CH))

    def layer3_pair(g):
        rows = (R * g, 12 - R * g)
        from_right = column_taps(0, rows)
        from_left = column_taps(1, rows)
        for odd in range(2):
            k, row = 2 * g + odd, rows[odd]
            z = dot(u3[pl.ds(row + 16 * odd, R)].reshape(R * COLS, CH), w[3, 2 * odd])
            new = s[pl.ds(row + 2, R), :COLS] + spread_cols(z)
            part = slice(odd * R * 8, (odd + 1) * R * 8)
            new = jnp.concatenate(
                [
                    new[:, :8] + from_left[part].reshape(R, 8, CH),
                    new[:, 8 : COLS - 8],
                    new[:, COLS - 8 :] + from_right[part].reshape(R, 8, CH),
                ],
                axis=1,
            )
            s[pl.ds(row + 2, R), :COLS] = new
            fa[k] = norm_act(new, gain(4), None)

    def third_received(k):
        src, dst, dr, dc = third[k]
        received(dst, e3_s.at[k], e3_r.at[k], -dr, -dc)
        for (_, dst, ss, rs, dr, dc) in list(columns(k))[1::2]:
            received(dst, ss, rs, -dr, -dc)

    weights_here(3)
    loop(4, layer3_own)
    weights_here(4)
    weights_here(5)

    for k in range(4):
        for (_, dst, ss, rs, dr, dc) in list(columns(k))[0::2]:
            received(dst, ss, rs, -dr, -dc)

    def far_send(k):
        move(k, True, "send", fa, fr, fa_s, fa_r)

    def far_sent(k):
        move(k, True, "sent", fa, fr, fa_s, fa_r)

    def layer3_turn(g):
        for turn in range(2):
            @pl.when(g == turn)
            def _():
                third_received(2 * turn)
                third_received(2 * turn + 1)

        @pl.when(g == 1)
        def _():
            far_send(0)
            far_send(1)

        layer3_pair(g)

    loop(2, layer3_turn)
    for k in (2, 3):
        far_send(k)

    def far_step(k):
        row = row_of(k)
        move(k, True, "received", fa, fr, fa_s, fa_r)
        left_side = jnp.concatenate(
            [v.reshape(R * COLS, CH) for v in (fr[k, 0], fa[k], fr[k, 1])], axis=-1
        )
        weight = wf[lax.rem(k, 2)].reshape(3 * CH, 3 * CH)
        z = dot(left_side, weight[:, : 2 * CH])
        fp[k, 0] = z[:, :CH].astype(jnp.bfloat16).reshape(R, COLS, CH)
        fp[k, 1] = z[:, CH :].astype(jnp.bfloat16).reshape(R, COLS, CH)
        move(k, False, "send", fp, fq, fp_s, fp_r)
        add(row, dot(left_side, weight[:, 2 * CH :]).reshape(R, COLS, CH))

    loop(4, far_step)

    def far_end(k):
        row = row_of(k)
        move(k, False, "received", fp, fq, fp_s, fp_r)
        far_sum = fq[k, 0].astype(jnp.float32) + fq[k, 1].astype(jnp.float32)
        out[pl.ds(row, R)] = s[pl.ds(row + 2, R), :COLS] + far_sum

    loop(4, far_end)

    for k, (src, dst, dr, dc) in enumerate(first):
        sent(src, dst, e0_s.at[k], e0_r.at[k], dr, dc)
    for k, (src, dst, dr, dc) in enumerate(second):
        sent(src, dst, e2_s.at[k], e2_r.at[k], dr, dc)
    for k, (src, dst, dr, dc) in enumerate(third):
        sent(src, dst, e3_s.at[k], e3_r.at[k], dr, dc)
        for args in columns(k):
            sent(*args)

    def all_sent(k):
        far_sent(k)
        move(k, False, "sent", fp, fq, fp_s, fp_r)

    loop(4, all_sent)


def local(nrow, ncol, features, inner_weights, far_weights, gains):
    bf16, f32 = jnp.bfloat16, jnp.float32
    dma = pltpu.SemaphoreType.DMA
    hbm = pl.BlockSpec(memory_space=pltpu.HBM)
    return pl.pallas_call(
        functools.partial(kernel, nrow, ncol),
        out_shape=jax.ShapeDtypeStruct(features.shape, f32),
        in_specs=[hbm] * 4,
        out_specs=pl.BlockSpec(memory_space=pltpu.VMEM),
        scratch_shapes=[
            pltpu.VMEM(gains.shape, f32),
            pltpu.VMEM((ROWS + 8, WIDE, CH), bf16),
            pltpu.VMEM((2, ROWS * 8, CH), bf16),
            pltpu.VMEM((2, (ROWS + 8) * 8, CH), bf16),
            pltpu.VMEM((ROWS + 8, WIDE, CH), bf16),
            pltpu.VMEM((ROWS + 4, WIDE, CH), bf16),
            pltpu.VMEM((ROWS + 8, WIDE, CH), bf16),
            pltpu.VMEM((ROWS + 16, COLS, CH), bf16),
            pltpu.VMEM((2, ROWS * 8, CH), bf16),
            pltpu.VMEM((2, (ROWS + 16) * 8, CH), bf16),
            pltpu.VMEM((ROWS + 4, WIDE, CH), f32),
            pltpu.VMEM((3 * R, 16, 3 * CH), f32),
            pltpu.VMEM((4, 3, CH, 3 * CH), bf16),
            pltpu.VMEM((2, 3, CH, 3 * CH), bf16),
            pltpu.VMEM((4, R, COLS, CH), bf16),
            pltpu.VMEM((4, 2, R, COLS, CH), bf16),
            pltpu.VMEM((4, 2, R, COLS, CH), bf16),
            pltpu.VMEM((4, 2, R, COLS, CH), bf16),
            dma, dma, dma((6,)),
            dma((8,)), dma((8,)), dma((2,)), dma((2,)), dma((4,)), dma((4,)),
            dma((4, 2)), dma((4, 2)), dma((4, 2)), dma((4, 2)), dma((4, 2)), dma((4, 2)), dma((4, 2)), dma((4, 2)),
        ],
        compiler_params=pltpu.CompilerParams(
            collective_id=0, has_side_effects=True, vmem_limit_bytes=50 * 2**20
        ),
    )(features, inner_weights, far_weights, gains)


def solution(mesh):
    return jax.shard_map(
        functools.partial(local, mesh.shape["row"], mesh.shape["col"]),
        mesh=mesh,
        in_specs=(P("row", "col", None), P(), P(), P()),
        out_specs=P("row", "col", None),
        check_vma=False,
    )
```
